512 devices in a mesh: row: 32 (over y_hi, z), col: 16 (over y_lo, x, core).
Axes of the slice: x: 4, y: 8 (y_hi: 4, y_lo: 2; y = y_hi * 2 + y_lo), z: 8, core: 2. Of those that a mesh axis runs over, the one named last changes fastest.
Arguments:
- features: bfloat16 [65536, 256], P(('col', 'row')), may hold values from -6 to 6
- weight: bfloat16 [256, 256], replicated, may hold values from -0.375 to 0.375
- cotangent: bfloat16 [65536, 256], P(('row', 'col')), may hold values from -6 to 6
- degrees: int32 [65536], replicated, may hold values from 0 to 63
- adj_blocks: bfloat16 [32, 16, 128, 128, 128], P('row', 'col'), may hold values from 0 to 0.046875
- block_rows: int32 [32, 16, 128], P('row', 'col'), may hold values from 0 to 15, as said below
- block_cols: int32 [32, 16, 128], P('row', 'col'), may hold values from 0 to 31
- block_count: int32 [32, 16], P('row', 'col'), may hold values from 16 to 128, as said below
Outputs:
- activations: bfloat16 [65536, 256], P(('row', 'col'))
- feature_grad: bfloat16 [65536, 256], P(('col', 'row'))
- weight_grad: float32 [256, 256], replicated
The draws below stay inside these ranges and needn't reach their ends.
Inputs may be any that keep to these rules, and one draw needn't show every extreme that they name: Within one tile the pairs (block_rows, block_cols) of its 128 slots are all different. `block_count`: every tile whose first row node lies in its column range uses all 128 slots.
All inputs are finite; a program needn't handle non-finite values.
Results may differ from the reference program's by a relative error of at most 0.027.
Values may be sent and summed in bfloat16 or wider, within the bound.
A program may use at most 64 MiB of HBM per device.

```python
from functools import partial
import jax
import jax.numpy as jnp
from jax import lax

F = 256
BS = 128
NODES = 65536
ROW_TILE = 2048
COL_TILE = 4096
ROW_BLOCKS = 16
COL_BLOCKS = 32
CAP = 128
N_ROW = 32
N_COL = 16


def slot_positions(key):
    keys = jax.random.split(jax.random.fold_in(key, 5), N_ROW * N_COL)
    chosen = jax.vmap(lambda tile_key: jax.random.permutation(tile_key, ROW_BLOCKS * COL_BLOCKS)[:CAP])(keys)
    return chosen.reshape(N_ROW, N_COL, CAP).astype(jnp.int32)


def draw_block_rows(key, part):
    return slot_positions(key) // COL_BLOCKS


def draw_block_cols(key, part):
    return slot_positions(key) % COL_BLOCKS


def draw_block_count(key, part):
    key = jax.random.fold_in(key, 11)
    tile_row = jnp.arange(N_ROW, dtype=jnp.int32)[:, None]
    tile_col = jnp.arange(N_COL, dtype=jnp.int32)[None, :]
    inside = tile_row * ROW_TILE // COL_TILE == tile_col
    lower = jax.random.randint(key, (N_ROW, N_COL), CAP // 8, CAP // 2 + 1, dtype=jnp.int32)
    return jnp.where(inside, jnp.int32(CAP), lower).astype(jnp.int32)


def plant(array, rng, smallest, high):
    longest = array.shape.index(max(array.shape))
    spots = []
    for shift in (0, 1):
        where = [jax.random.randint(jax.random.fold_in(rng, axis), (), 0, length) for axis, length in enumerate(array.shape)]
        where[longest] = (where[longest] + shift) % array.shape[longest]
        spots.append(tuple(where))
    return array.at[spots[0]].set(smallest).at[spots[1]].set(high)


def block_scale(own_key, shape, cuts, least, top_value):
    level, own = 1.0, jax.random.fold_in(own_key, 6)
    for dim, blocks in cuts:
        steps = jnp.exp(jax.random.uniform(jax.random.fold_in(own, dim), (blocks,), jnp.float32, least / len(cuts), top_value / len(cuts)))
        level = level * jnp.repeat(steps, shape[dim] // blocks).reshape([-1 if axis == dim else 1 for axis in range(len(shape))])
    return level


def centred(stream_key, dims, deviation, reach, shards=(), kind=jnp.bfloat16):
    level = block_scale(stream_key, dims, shards, -0.22, 0.18) if shards else 1.0
    drawn = jax.random.normal(stream_key, dims, jnp.float32) * deviation * level
    return jnp.minimum(jnp.maximum(drawn, -reach), reach).astype(kind)


def setup_inputs(seed: int = 0) -> dict:
    key_of = jax.random.split(jax.random.key(seed), 9)
    features = centred(key_of[0], (NODES, F), 1.0, 6.0, ((0, 512),))
    weight = centred(key_of[1], (F, F), F ** -0.5, 0.375)
    cotangent = centred(key_of[2], (NODES, F), 1.0, 6.0, ((0, 512),))
    degrees = plant(jax.random.randint(key_of[3], (NODES,), 0, 64), jax.random.fold_in(key_of[3], 1), 0, 63).astype(jnp.int32)
    adj_blocks = jnp.clip(0.046875 * jax.random.uniform(key_of[4], (N_ROW, N_COL, CAP, BS, BS), jnp.float32) ** block_scale(key_of[4], (N_ROW, N_COL, CAP, BS, BS), ((0, 32), (1, 16)), -0.2, 0.2), 0.0, 0.046875).astype(jnp.bfloat16)
    block_rows = draw_block_rows(jax.random.fold_in(key_of[8], 71), 0)
    block_cols = draw_block_cols(jax.random.fold_in(key_of[8], 71), 0)
    block_count = draw_block_count(jax.random.fold_in(key_of[8], 71), 0)
    return dict(features=features, weight=weight, cotangent=cotangent, degrees=degrees, adj_blocks=adj_blocks, block_rows=block_rows, block_cols=block_cols, block_count=block_count)


def degree_scale(degrees):
    safe = jnp.maximum(degrees, 1).astype(jnp.float32)
    return jnp.where(degrees > 0, lax.rsqrt(safe), jnp.float32(0.0))

def tile_forward(blocks, brows, bcols, count, source):
    pieces = source.reshape(COL_BLOCKS, BS, F)
    picked = pieces[bcols].astype(jnp.float32)
    products = jnp.einsum('kab,kbf->kaf', blocks.astype(jnp.float32), picked)
    alive = jnp.arange(CAP) < count
    onehot = ((brows[None, :] == jnp.arange(ROW_BLOCKS)[:, None]) & alive[None, :]).astype(jnp.float32)
    summed = jnp.einsum('rk,kaf->raf', onehot, products, precision=lax.Precision.HIGHEST)
    return summed.reshape(ROW_TILE, F)

def tile_backward(blocks, brows, bcols, count, source):
    pieces = source.reshape(ROW_BLOCKS, BS, F)
    picked = pieces[brows].astype(jnp.float32)
    products = jnp.einsum('kba,kbf->kaf', blocks.astype(jnp.float32), picked)
    alive = jnp.arange(CAP) < count
    onehot = ((bcols[None, :] == jnp.arange(COL_BLOCKS)[:, None]) & alive[None, :]).astype(jnp.float32)
    summed = jnp.einsum('rk,kaf->raf', onehot, products, precision=lax.Precision.HIGHEST)
    return summed.reshape(COL_TILE, F)

def rounded(value):
    low = lax.optimization_barrier(value.astype(jnp.bfloat16))
    return low.astype(jnp.float32)

def reference(features, weight, cotangent, degrees, adj_blocks, block_rows, block_cols, block_count):
    scale = degree_scale(degrees)
    scaled = (features.astype(jnp.float32) * scale[:, None]).astype(jnp.bfloat16)
    col_sources = scaled.reshape(N_COL, COL_TILE, F)

    def row_tile(tile_row):

        def add_tile(total, tile_col):
            term = tile_forward(adj_blocks[tile_row, tile_col], block_rows[tile_row, tile_col], block_cols[tile_row, tile_col], block_count[tile_row, tile_col], col_sources[tile_col])
            return (total + rounded(term), None)
        total, unused = lax.scan(add_tile, jnp.zeros((ROW_TILE, F), jnp.float32), jnp.arange(N_COL))
        return total
    summed = lax.map(row_tile, jnp.arange(N_ROW)).reshape(NODES, F)
    propagated = (summed * scale[:, None]).astype(jnp.bfloat16)
    pre = jnp.dot(propagated, weight, preferred_element_type=jnp.float32)
    output, backward = jax.vjp(partial(jax.nn.gelu, approximate=True), pre)
    activations = output.astype(jnp.bfloat16)
    pre_grad = backward(cotangent.astype(jnp.float32))[0].astype(jnp.bfloat16)
    weight_grad = jnp.dot(propagated.T, pre_grad, preferred_element_type=jnp.float32)
    back_full = lax.dot_general(pre_grad, weight, (((1,), (1,)), ((), ())), preferred_element_type=jnp.float32)
    back_scaled = (back_full * scale[:, None]).astype(jnp.bfloat16)
    row_sources = back_scaled.reshape(N_ROW, ROW_TILE, F)

    def col_tile(tile_col):

        def add_tile(total, tile_row):
            term = tile_backward(adj_blocks[tile_row, tile_col], block_rows[tile_row, tile_col], block_cols[tile_row, tile_col], block_count[tile_row, tile_col], row_sources[tile_row])
            return (total + rounded(term), None)
        total, unused = lax.scan(add_tile, jnp.zeros((COL_TILE, F), jnp.float32), jnp.arange(N_ROW))
        return total
    back_sum = lax.map(col_tile, jnp.arange(N_COL)).reshape(NODES, F)
    feature_grad = (back_sum * scale[:, None]).astype(jnp.bfloat16)
    return (activations, feature_grad, weight_grad)
```

```python
import math

import jax
import jax.numpy as jnp
from jax import lax
from jax.experimental import pallas as pl
from jax.experimental.pallas import tpu as pltpu
from jax.sharding import PartitionSpec as P

NY, NZ = 4, 8
NX, NL = 4, 2
CHIPS = NX * NL
BS = 128
F = 256
CAP = 128
BF, F32, I32 = jnp.bfloat16, jnp.float32, jnp.int32
MESH = pl.DeviceIdType.MESH

GELU_A = math.sqrt(2.0 / math.pi)
GELU_B = 0.044715

GATHER_ORDER = (0, 1, 3, 2)
SCATTER_ORDER = (2, 1, 3, 0)
CHIP_ORDER = ((1, 2), (1, 1), (1, 3), (1, 0), (0, 2), (0, 1), (0, 3), (0, 0))


def scale_of(degrees):
    safe = jnp.maximum(degrees, 1).astype(F32)
    return jnp.where(degrees > 0, lax.rsqrt(safe), jnp.float32(0.0))


def down_rows(line, width):
    square = jnp.broadcast_to(line, (BS, BS)).T
    return jnp.concatenate([square] * (width // BS), axis=1) if width > BS else square


def gather_has(way, step, d):
    return step < 3 or (step == 3 and (d in (0, 1)) == (way == 0))


def scatter_has(way, step, d):
    return step > 0 or (d in (2, 0)) == (way == 0)


def kernel(
    feat, weight, cot, deg, adj, brow, bcol, cnt,
    act_out, fg_out, wg_out,
    blocks, turned, src, acc, inv_v, inv_s,
    pair_out, pair_in, chip_out, chip_in, grads,
    part, ring_out, ring_in, last_out, last_in,
    w_half_out, w_half_in, w_piece_out, w_piece_in, w_z, w_y, w_all, w_other,
    adj_sem, inv_sem, gy_s, gy_r, gz_s, gz_r, pair_s, pair_r, chip_s, chip_r,
    ag_s, ag_r, fw_s, fw_r, rz_s, rz_r, ry_s, ry_r,
    wh_s, wh_r, wp_s, wp_r, wz_s, wz_r, wy_s, wy_r, wa_s, wa_r, wo_s, wo_r,
):
    row = lax.axis_index("row")
    col = lax.axis_index("col")
    y, z = row // NZ, row % NZ
    chip, core = col // 2, col % 2
    ylo, x = chip // NX, chip % NX

    def at_z(k):
        return (y * NZ + (z + k + NZ) % NZ, col)

    def at_y(d):
        return (((y + d) % NY) * NZ + z, col)

    def chip_at(k):
        dl, dx = CHIP_ORDER[k]
        return ((ylo + dl) % NL) * NX + (x + dx) % NX

    def chip_from(k):
        dl, dx = CHIP_ORDER[k]
        return ((ylo + NL - dl) % NL) * NX + (x + NX - dx) % NX

    def at_chip(k):
        return (row, chip_at(k) * 2 + core)

    sibling = (row, chip * 2 + 1 - core)

    adj_copy = pltpu.make_async_copy(adj, blocks.at[pl.ds(0, CAP)], adj_sem)
    adj_copy.start()

    barrier = pltpu.get_barrier_semaphore()
    partners = [at_z(k) for k in range(1, NZ)] + [at_y(d) for d in range(1, NY)]
    partners += [at_chip(k) for k in range(CHIPS - 1)] + [sibling]
    for partner in partners:
        pl.semaphore_signal(barrier, inc=1, device_id=partner, device_id_type=MESH)

    own_scale = down_rows(scale_of(deg[pl.ds(col * (NY * NZ) + row, 1), :]), F)
    src[row] = (feat[...].astype(F32) * own_scale).astype(BF)

    pl.semaphore_wait(barrier, len(partners))

    started = []

    def send(source, target, send_sem, recv_sem, device):
        copy = pltpu.make_async_remote_copy(
            src_ref=source, dst_ref=target, send_sem=send_sem, recv_sem=recv_sem,
            device_id=device, device_id_type=MESH,
        )
        copy.start()
        started.append(copy)

    def arrived(buffer, recv_sem):
        pltpu.make_async_remote_copy(
            src_ref=buffer, dst_ref=buffer, send_sem=recv_sem, recv_sem=recv_sem,
            device_id=sibling, device_id_type=MESH,
        ).wait_recv()

    def origin(way, step, d):
        zz = (z - step + NZ) % NZ if way == 0 else (z + step) % NZ
        return ((y + NY - d) % NY) * NZ + zz

    def pass_on(way, step, d):
        ref = src.at[origin(way, step, d)]
        send(ref, ref, gz_s.at[way, step, d], gz_r.at[way, step, d], at_z(1 if way == 0 else -1))

    for d in (1, 3, 2):
        send(src.at[row], src.at[row], gy_s.at[d], gy_r.at[d], at_y(d))
    for way in (0, 1):
        pass_on(way, 0, 0)

    lane = lax.broadcasted_iota(I32, (1, BS), 1)
    place = jnp.where(lane < cnt[0, 0], brow[...] * 32 + bcol[...], -1)
    place = jnp.broadcast_to(place, (BS, BS)).T
    slot = lax.broadcasted_iota(I32, (BS, BS), 0)
    spot = lax.broadcasted_iota(I32, (BS, BS), 1)
    for q in range(4):
        hit = jnp.where(place == spot + q * BS, slot - CAP, 0)
        inv_v[q : q + 1, :] = jnp.sum(hit, axis=0, keepdims=True) + CAP
    inv_v[4:8, :] = jnp.zeros((4, BS), I32)
    inv_copy = pltpu.make_async_copy(inv_v, inv_s, inv_sem)
    inv_copy.start()
    blocks[CAP] = jnp.zeros((BS, BS), BF)
    turned[CAP] = jnp.zeros((BS, BS), BF)

    for d in (1, 3, 2):
        arrived(src.at[origin(0, 0, d)], gy_r.at[d])
        for way in (0, 1):
            pass_on(way, 0, d)

    def lookup(r, c):
        return inv_s[r // 4, (r % 4) * 32 + c]

    def strip(z_at):
        return jnp.concatenate([src[yy * NZ + z_at] for yy in range(NY)], axis=0)

    def tile_rows(rows, z_at):
        return jnp.concatenate(
            [
                jnp.concatenate([blocks[lookup(r, yy * NZ + z_at)] for yy in range(NY)], axis=1)
                for r in rows
            ],
            axis=0,
        )

    def add_strip(z_at, first):
        def some(g, carry):
            out = jnp.dot(
                tile_rows([g * 4 + i for i in range(4)], z_at), strip(z_at),
                preferred_element_type=F32,
            ).reshape(4, BS, F)
            if first:
                acc[pl.ds(g * 4, 4)] = out
            else:
                acc[pl.ds(g * 4, 4)] += out
            return carry

        lax.fori_loop(0, 4, some, 0)

    def turn(first, last):
        def one(k, carry):
            turned[k] = blocks[k].T
            return carry

        lax.fori_loop(first, last, one, 0)

    adj_copy.wait()
    inv_copy.wait()
    add_strip(z, True)

    for step in range(4):
        for d in GATHER_ORDER:
            for way in (0, 1):
                if gather_has(way, step, d):
                    arrived(src.at[origin(way, step + 1, d)], gz_r.at[way, step, d])
                    if gather_has(way, step + 1, d):
                        pass_on(way, step + 1, d)
        if step < 3:
            add_strip((z + NZ - step - 1) % NZ, False)
            add_strip((z + step + 1) % NZ, False)
            turn(step * CAP // 3, (step + 1) * CAP // 3)

    far = (z + 4) % NZ
    for ours in (False, True):
        which = core if ours else 1 - core
        for g in (0, 1):
            ks = range(g * 4, g * 4 + 4)
            rows = [chip_at(k) * 2 + which for k in ks]
            out = jnp.dot(tile_rows(rows, far), strip(far), preferred_element_type=F32)
            for i, k in enumerate(ks):
                total = acc[rows[i]] + out[i * BS : (i + 1) * BS]
                if ours:
                    acc[rows[i]] = total
                else:
                    pair_out[k] = total.astype(BF)
            if not ours:
                group = pl.ds(g * 4, 4)
                send(pair_out.at[group], pair_in.at[group], pair_s.at[g], pair_r.at[g], sibling)
    for g in (0, 1):
        group = pl.ds(g * 4, 4)
        arrived(pair_in.at[group], pair_r.at[g])
        for k in range(g * 4, g * 4 + 4):
            total = acc[chip_at(k) * 2 + core] + pair_in[k].astype(F32)
            if k < CHIPS - 1:
                chip_out[k] = total.astype(BF)
                send(chip_out.at[k], chip_in.at[k], chip_s.at[k], chip_r.at[k], at_chip(k))
    for k in reversed(range(CHIPS - 1)):
        arrived(chip_in.at[k], chip_r.at[k])
        total = total + chip_in[k].astype(F32)

    row_scale = down_rows(scale_of(deg[pl.ds(row * (CHIPS * 2) + col, 1), :]), F)
    propagated = (total * row_scale).astype(BF)
    pre = jnp.dot(propagated, weight[...], preferred_element_type=F32)
    square = pre * pre
    tanh = jnp.tanh(GELU_A * (pre + GELU_B * (square * pre)))
    cdf = 0.5 * (1.0 + tanh)
    slope = cdf + 0.5 * pre * (1.0 - tanh * tanh) * (GELU_A * (1.0 + 3.0 * GELU_B * square))
    pre_grad = (cot[...].astype(F32) * slope).astype(BF)
    back = lax.dot_general(
        pre_grad, weight[...], (((1,), (1,)), ((), ())), preferred_element_type=F32
    )
    grads[col] = (back * row_scale).astype(BF)

    mine = grads.at[col]
    for k in range(CHIPS - 1):
        send(mine, mine, ag_s.at[k], ag_r.at[k], at_chip(k))
    send(mine, mine, fw_s.at[CHIPS - 1], fw_r.at[CHIPS - 1], sibling)

    act_out[...] = (pre * cdf).astype(BF)
    w_local = lax.dot_general(
        propagated, pre_grad, (((0,), (0,)), ((), ())), preferred_element_type=F32
    )
    part[0] = w_local[0:BS]
    part[1] = w_local[BS:F]
    w_half_out[...] = part[1 - core].astype(BF)
    send(w_half_out, w_half_in, wh_s, wh_r, sibling)

    for k in reversed(range(CHIPS - 1)):
        ref = grads.at[chip_from(k) * 2 + core]
        arrived(ref, ag_r.at[k])
        send(ref, ref, fw_s.at[k], fw_r.at[k], sibling)

    arrived(w_half_in, wh_r)
    half = part[core] + w_half_in[...].astype(F32)
    for c in range(CHIPS):
        w_piece_out[c] = half[c * 16 : (c + 1) * 16].astype(BF)
    for k in range(CHIPS - 1):
        send(w_piece_out.at[chip_at(k)], w_piece_in.at[k], wp_s.at[k], wp_r.at[k], at_chip(k))

    for k in reversed(range(CHIPS)):
        arrived(grads.at[chip_from(k) * 2 + 1 - core], fw_r.at[k])

    def back_strip(z_at, target):
        lhs = jnp.concatenate(
            [
                jnp.concatenate(
                    [turned[lookup(r, ((y + d) % NY) * NZ + z_at)] for r in range(16)], axis=1
                )
                for d in range(NY)
            ],
            axis=0,
        )
        out = jnp.dot(lhs, grads[...].reshape(16 * BS, F), preferred_element_type=F32)
        part[pl.ds(target * NY, NY)] = out.reshape(NY, BS, F)

    def w_step(step):
        if step == 0:
            total = w_piece_out[chip].astype(F32)
            for k in range(CHIPS - 1):
                arrived(w_piece_in.at[k], wp_r.at[k])
                total = total + w_piece_in[k].astype(F32)
            w_z[z] = total.astype(BF)
            for k in range(1, NZ):
                send(w_z.at[z], w_z.at[z], wz_s.at[k], wz_r.at[k], at_z(k))
        if step == 1:
            for k in range(1, NZ):
                arrived(w_z.at[(z + NZ - k) % NZ], wz_r.at[k])
            total = w_z[0].astype(F32)
            for k in range(1, NZ):
                total = total + w_z[k].astype(F32)
            w_y[y] = total.astype(BF)
            for d in range(1, NY):
                send(w_y.at[y], w_y.at[y], wy_s.at[d], wy_r.at[d], at_y(d))
        if step == 2:
            for d in range(1, NY):
                arrived(w_y.at[(y + NY - d) % NY], wy_r.at[d])
            total = w_y[0].astype(F32)
            for d in range(1, NY):
                total = total + w_y[d].astype(F32)
            w_all[chip] = total.astype(BF)
            for k in range(CHIPS - 1):
                send(w_all.at[chip], w_all.at[chip], wa_s.at[k], wa_r.at[k], at_chip(k))
        if step == 3:
            for k in range(CHIPS - 1):
                arrived(w_all.at[chip_from(k)], wa_r.at[k])
            send(w_all, w_other, wo_s, wo_r, sibling)

    back_strip((z + 4) % NZ, 0)
    for step in range(4):
        for d in SCATTER_ORDER:
            for way in (0, 1):
                if not scatter_has(way, step, d):
                    continue
                value = part[(way if step else 0) * NY + d]
                if step and scatter_has(way, step - 1, d):
                    arrived(ring_in.at[way, step - 1, d], rz_r.at[way, step - 1, d])
                    value = value + ring_in[way, step - 1, d].astype(F32)
                ring_out[way, step, d] = value.astype(BF)
                send(
                    ring_out.at[way, step, d], ring_in.at[way, step, d],
                    rz_s.at[way, step, d], rz_r.at[way, step, d], at_z(1 if way == 0 else -1),
                )
        if step < 3:
            back_strip((z + 3 - step) % NZ, 0)
            back_strip((z + NZ - 3 + step) % NZ, 1)
        else:
            back_strip(z, 0)
        w_step(step)

    for d in SCATTER_ORDER:
        value = part[d]
        for way in (0, 1):
            arrived(ring_in.at[way, 3, d], rz_r.at[way, 3, d])
            value = value + ring_in[way, 3, d].astype(F32)
        if d:
            last_out[d] = value.astype(BF)
            send(last_out.at[d], last_in.at[d], ry_s.at[d], ry_r.at[d], at_y(d))

    arrived(w_other, wo_r)
    wg_out[pl.ds(pl.multiple_of(core * BS, BS), BS), :] = w_all[...].astype(F32).reshape(BS, F)
    wg_out[pl.ds(pl.multiple_of((1 - core) * BS, BS), BS), :] = (
        w_other[...].astype(F32).reshape(BS, F)
    )

    for d in (1, 3, 2):
        arrived(last_in.at[d], ry_r.at[d])
        value = value + last_in[d].astype(F32)
    fg_out[...] = (value * own_scale).astype(BF)

    for copy in started:
        copy.wait_send()


def per_device(
    features, weight, cotangent, degrees, adj_blocks, block_rows, block_cols, block_count
):
    vmem = pl.BlockSpec(memory_space=pltpu.VMEM)
    dma = pltpu.SemaphoreType.DMA
    block = (BS, F)
    scratch = [
        pltpu.VMEM((CAP + 1, BS, BS), BF),
        pltpu.VMEM((CAP + 1, BS, BS), BF),
        pltpu.VMEM((NY * NZ,) + block, BF),
        pltpu.VMEM((CHIPS * 2,) + block, F32),
        pltpu.VMEM((8, BS), I32),
        pltpu.SMEM((8, BS), I32),
        pltpu.VMEM((CHIPS,) + block, BF),
        pltpu.VMEM((CHIPS,) + block, BF),
        pltpu.VMEM((CHIPS,) + block, BF),
        pltpu.VMEM((CHIPS,) + block, BF),
        pltpu.VMEM((CHIPS * 2,) + block, BF),
        pltpu.VMEM((2 * NY,) + block, F32),
        pltpu.VMEM((2, 4, NY) + block, BF),
        pltpu.VMEM((2, 4, NY) + block, BF),
        pltpu.VMEM((NY,) + block, BF),
        pltpu.VMEM((NY,) + block, BF),
        pltpu.VMEM(block, BF),
        pltpu.VMEM(block, BF),
        pltpu.VMEM((CHIPS, 16, F), BF),
        pltpu.VMEM((CHIPS, 16, F), BF),
        pltpu.VMEM((NZ, 16, F), BF),
        pltpu.VMEM((NY, 16, F), BF),
        pltpu.VMEM((CHIPS, 16, F), BF),
        pltpu.VMEM((CHIPS, 16, F), BF),
    ]
    sems = [dma, dma]
    for shape in (
        (NY,), (2, 4, NY), (2,), (CHIPS,), (CHIPS,), (CHIPS,), (2, 4, NY), (NY,),
        None, (CHIPS,), (NZ,), (NY,), (CHIPS,), None,
    ):
        sems += [dma if shape is None else dma(shape)] * 2
    return pl.pallas_call(
        kernel,
        out_shape=(
            jax.ShapeDtypeStruct(block, BF),
            jax.ShapeDtypeStruct(block, BF),
            jax.ShapeDtypeStruct((F, F), F32),
        ),
        in_specs=[vmem, vmem, vmem, vmem, pl.BlockSpec(memory_space=pl.ANY), vmem, vmem]
        + [pl.BlockSpec(memory_space=pltpu.SMEM)],
        out_specs=(vmem, vmem, vmem),
        scratch_shapes=scratch + sems,
        compiler_params=pltpu.CompilerParams(
            collective_id=0, has_side_effects=True, vmem_limit_bytes=48 * 1024 * 1024
        ),
        cost_estimate=pl.CostEstimate(
            flops=8 * 2048 * 4096 * 256 // 2, bytes_accessed=5 * 1024 * 1024, transcendentals=32768
        ),
        name="layer",
    )(
        features,
        weight,
        cotangent,
        degrees.reshape(-1, BS),
        adj_blocks.reshape(CAP, BS, BS),
        block_rows.reshape(1, CAP),
        block_cols.reshape(1, CAP),
        block_count,
    )


def solution(mesh):
    in_specs = (
        P(("col", "row"), None),
        P(),
        P(("row", "col"), None),
        P(),
        P("row", "col", None, None, None),
        P("row", "col", None),
        P("row", "col", None),
        P("row", "col"),
    )
    out_specs = (P(("row", "col"), None), P(("col", "row"), None), P())
    return jax.shard_map(
        per_device, mesh=mesh, in_specs=in_specs, out_specs=out_specs, check_vma=False
    )
```

```python
import math

import jax
import jax.numpy as jnp
from jax import lax
from jax.experimental import pallas as pl
from jax.experimental.pallas import tpu as pltpu
from jax.sharding import PartitionSpec as P

NY, NZ = 4, 8
NX, NL = 4, 2
CHIPS = NX * NL
BS = 128
F = 256
CAP = 128
BF, F32, I32 = jnp.bfloat16, jnp.float32, jnp.int32
MESH = pl.DeviceIdType.MESH

GELU_A = math.sqrt(2.0 / math.pi)
GELU_B = 0.044715

TALL = 96
G_PIECES, S_PIECES = 1, 1
G_ROWS, S_ROWS = TALL // G_PIECES, TALL // S_PIECES
GATHER = (
    ("z", 0, 0, 0, 0), ("z", 0, 1, 0, 0), ("b", 0, 0), ("b", 1, 0), ("y", 0, 1), ("y", 0, 3),
    ("z", 0, 0, 1, 0), ("z", 0, 1, 1, 0), ("b", 0, 1), ("b", 1, 1), ("z", 0, 0, 0, 1), ("y", 0, 2),
    ("z", 0, 1, 0, 1), ("q", 0, 1), ("q", 0, 3), ("q", 0, 2), ("c", 0), ("z", 0, 0, 0, 3),
    ("z", 0, 1, 0, 3), ("q", 1, 1), ("q", 1, 3), ("z", 0, 0, 2, 0), ("q", 1, 2), ("z", 0, 1, 2, 0),
    ("b", 0, 2), ("b", 1, 2), ("q", 5, 1), ("q", 5, 3), ("z", 0, 0, 1, 1), ("q", 5, 2),
    ("z", 0, 1, 0, 2), ("c", 5), ("z", 0, 0, 0, 2), ("q", 2, 1), ("c", 1), ("q", 2, 3),
    ("z", 0, 1, 1, 1), ("q", 2, 2), ("z", 0, 0, 1, 3), ("z", 0, 1, 1, 3), ("q", 6, 1), ("q", 6, 3),
    ("q", 6, 2), ("z", 0, 0, 3, 0), ("z", 0, 1, 1, 2), ("c", 6), ("b", 0, 3), ("q", 3, 1),
    ("q", 3, 3), ("q", 3, 2), ("z", 0, 0, 2, 1), ("z", 0, 1, 2, 1), ("q", 7, 1), ("q", 7, 3),
    ("z", 0, 0, 1, 2), ("q", 7, 2), ("c", 2), ("z", 0, 1, 2, 3), ("z", 0, 0, 2, 3),
    ("z", 0, 1, 2, 2), ("c", 7), ("z", 0, 0, 3, 1), ("q", 4, 1), ("q", 4, 3), ("q", 4, 2),
    ("z", 0, 0, 2, 2), ("c", 3), ("z", 0, 1, 3, 3), ("z", 0, 1, 3, 2),
)
SCATTER = (
    ("c", 4), ("z", 0, 0, 0, 2), ("z", 0, 1, 0, 1), ("z", 0, 1, 0, 3), ("z", 0, 0, 0, 0), ("q", 4),
    ("c", 3), ("z", 0, 0, 1, 1), ("z", 0, 0, 1, 3), ("q", 3), ("c", 7), ("z", 0, 1, 1, 2),
    ("z", 0, 1, 1, 0), ("q", 7), ("z", 0, 0, 1, 2), ("z", 0, 1, 1, 1), ("c", 2), ("q", 2), ("w", 0),
    ("z", 0, 1, 1, 3), ("z", 0, 0, 1, 0), ("c", 6), ("b", 0, 0), ("z", 0, 0, 2, 1), ("q", 6),
    ("z", 0, 1, 2, 2), ("c", 1), ("z", 0, 0, 2, 3), ("q", 1), ("z", 0, 1, 2, 0), ("c", 5),
    ("z", 0, 0, 2, 2), ("w", 1), ("q", 5), ("b", 1, 1), ("z", 0, 1, 2, 1), ("z", 0, 0, 2, 0),
    ("c", 0), ("b", 0, 1), ("z", 0, 1, 2, 3), ("q", 0), ("z", 0, 0, 3, 1), ("z", 0, 1, 3, 2),
    ("z", 0, 0, 3, 3), ("z", 0, 1, 3, 0), ("w", 2), ("b", 1, 2), ("z", 0, 0, 3, 2),
    ("z", 0, 1, 3, 1), ("z", 0, 0, 3, 0), ("b", 0, 2), ("z", 0, 1, 3, 3), ("w", 3), ("b", 1, 3),
    ("y", 0, 2), ("y", 0, 1), ("b", 0, 3), ("y", 0, 3), ("s",), ("t", 0),
)
CHIP_ORDER = ((1, 2), (1, 1), (1, 3), (1, 0), (0, 2), (0, 1), (0, 3), (0, 0))


def scale_of(degrees):
    safe = jnp.maximum(degrees, 1).astype(F32)
    return jnp.where(degrees > 0, lax.rsqrt(safe), jnp.float32(0.0))


def down_rows(line, width):
    square = jnp.broadcast_to(line, (BS, BS)).T
    return jnp.concatenate([square] * (width // BS), axis=1) if width > BS else square


def short_has(way, step):
    return step < 3 or (step == 3 and way == 0)


def short_at(way, step):
    return 1 + step + 4 * way


def gather_has(way, step, d):
    return step < 3 or (step == 3 and (d in (0, 1)) == (way == 0))


def short_ring_has(way, step):
    return step > 0 or way == 0


def scatter_has(way, step, d):
    return step > 0 or (d in (2, 0)) == (way == 0)


def kernel(
    feat_h, weight_h, cot_h, deg_h, adj, brow_h, bcol_h, cnt_h,
    act_out, fg_out, wg_out,
    feat, weight, cot, deg, brow, bcol, cnt,
    blocks, turned, src, acc, inv_v, inv_s,
    pair_out, pair_in, chip_out, chip_in, grads,
    part, ring_out, ring_in, last_out, last_in,
    w_half_out, w_half_in, w_piece_out, w_piece_in, w_z, w_y, w_all, w_other,
    short_out, short_in, short_ring_out, short_ring_in,
    in_sem, adj_sem, inv_sem, gy_s, gy_r, gz_s, gz_r, pair_s, pair_r, chip_s, chip_r,
    ag_s, ag_r, fw_s, fw_r, rz_s, rz_r, ry_s, ry_r,
    wh_s, wh_r, wp_s, wp_r, wz_s, wz_r, wy_s, wy_r, wa_s, wa_r, wo_s, wo_r,
    hz_s, hz_r, hy_s, hy_r, kz_s, kz_r, ky_s, ky_r,
):
    row = lax.axis_index("row")
    col = lax.axis_index("col")
    y, z = row // NZ, row % NZ
    chip, core = col // 2, col % 2
    ylo, x = chip // NX, chip % NX

    def at_z(k):
        return (y * NZ + (z + k + NZ) % NZ, col)

    def at_y(d):
        return (((y + d) % NY) * NZ + z, col)

    def chip_at(k):
        dl, dx = CHIP_ORDER[k]
        return ((ylo + dl) % NL) * NX + (x + dx) % NX

    def chip_from(k):
        dl, dx = CHIP_ORDER[k]
        return ((ylo + NL - dl) % NL) * NX + (x + NX - dx) % NX

    def at_chip(k):
        return (row, chip_at(k) * 2 + core)

    sibling = (row, chip * 2 + 1 - core)

    loads = [
        pltpu.make_async_copy(source, target, in_sem.at[i])
        for i, (source, target) in enumerate(
            (
                (deg_h, deg), (feat_h, feat), (brow_h, brow), (bcol_h, bcol),
                (cnt_h, cnt), (weight_h, weight), (cot_h, cot),
            )
        )
    ]
    for load in loads:
        load.start()
    adj_copy = pltpu.make_async_copy(adj, blocks.at[pl.ds(0, CAP)], adj_sem)
    adj_copy.start()

    barrier = pltpu.get_barrier_semaphore()
    partners = [at_z(k) for k in range(1, NZ)] + [at_y(d) for d in range(1, NY)]
    partners += [at_chip(k) for k in range(CHIPS - 1)] + [sibling]
    for partner in partners:
        pl.semaphore_signal(barrier, inc=1, device_id=partner, device_id_type=MESH)

    for load in loads[:2]:
        load.wait()
    own_scale = down_rows(scale_of(deg[pl.ds(col * (NY * NZ) + row, 1), :]), F)
    src[row] = (feat[...].astype(F32) * own_scale).astype(BF)

    for load in loads[2:5]:
        load.wait()
    lane = lax.broadcasted_iota(I32, (1, BS), 1)
    place = jnp.where(lane < cnt[0, 0], brow[...] * 32 + bcol[...], -1)
    place = jnp.broadcast_to(place, (BS, BS)).T
    slot = lax.broadcasted_iota(I32, (BS, BS), 0)
    spot = lax.broadcasted_iota(I32, (BS, BS), 1)
    for q in range(4):
        hit = jnp.where(place == spot + q * BS, slot - CAP, 0)
        inv_v[q : q + 1, :] = jnp.sum(hit, axis=0, keepdims=True) + CAP
    inv_v[4:8, :] = jnp.zeros((4, BS), I32)
    inv_copy = pltpu.make_async_copy(inv_v, inv_s, inv_sem)
    inv_copy.start()
    blocks[CAP] = jnp.zeros((BS, BS), BF)
    turned[CAP] = jnp.zeros((BS, BS), BF)

    def turn(first, last):
        def one(k, carry):
            turned[k] = blocks[k].T
            return carry

        lax.fori_loop(first, last, one, 0)

    adj_copy.wait()
    turn(0, CAP // 2)
    pl.semaphore_wait(barrier, len(partners))

    started = []

    def send(source, target, send_sem, recv_sem, device):
        copy = pltpu.make_async_remote_copy(
            src_ref=source, dst_ref=target, send_sem=send_sem, recv_sem=recv_sem,
            device_id=device, device_id_type=MESH,
        )
        copy.start()
        started.append(copy)

    def arrived(buffer, recv_sem):
        pltpu.make_async_remote_copy(
            src_ref=buffer, dst_ref=buffer, send_sem=recv_sem, recv_sem=recv_sem,
            device_id=sibling, device_id_type=MESH,
        ).wait_recv()

    def origin(way, step, d):
        zz = (z - step + NZ) % NZ if way == 0 else (z + step) % NZ
        return ((y + NY - d) % NY) * NZ + zz

    def tall(r, c):
        return src.at[r, pl.ds(c * G_ROWS, G_ROWS)]

    def short(r):
        return src.at[r, pl.ds(TALL, BS - TALL)]

    def pass_on(c, way, step, d):
        ref = tall(origin(way, step, d), c)
        i = d * G_PIECES + c
        send(ref, ref, gz_s.at[way, step, i], gz_r.at[way, step, i], at_z(1 if way == 0 else -1))

    def short_pass_on(way, step):
        ref = short(origin(way, step, 0))
        send(ref, ref, hz_s.at[way, step], hz_r.at[way, step], at_z(1 if way == 0 else -1))

    def short_spread(i, r):
        for d in (2, 1, 3):
            send(short(r), short(r), hy_s.at[i, d], hy_r.at[i, d], at_y(d))

    for c in range(G_PIECES):
        for way in (0, 1):
            pass_on(c, way, 0, 0)
    for c in range(G_PIECES):
        for d in (1, 3, 2):
            i = d * G_PIECES + c
            send(tall(row, c), tall(row, c), gy_s.at[i], gy_r.at[i], at_y(d))
    for way in (0, 1):
        short_pass_on(way, 0)
    short_spread(0, row)

    def lookup(r, c):
        return inv_s[r // 4, (r % 4) * 32 + c]

    def strip(z_at):
        return jnp.concatenate([src[yy * NZ + z_at] for yy in range(NY)], axis=0)

    def tile_rows(rows, z_at):
        return jnp.concatenate(
            [
                jnp.concatenate([blocks[lookup(r, yy * NZ + z_at)] for yy in range(NY)], axis=1)
                for r in rows
            ],
            axis=0,
        )

    def add_strip(z_at, first):
        def some(g, carry):
            out = jnp.dot(
                tile_rows([g * 4 + i for i in range(4)], z_at), strip(z_at),
                preferred_element_type=F32,
            ).reshape(4, BS, F)
            if first:
                acc[pl.ds(g * 4, 4)] = out
            else:
                acc[pl.ds(g * 4, 4)] += out
            return carry

        lax.fori_loop(0, 4, some, 0)

    def strip_way(i):
        return (0, i) if i <= 4 else (1, i - 4)

    def strip_z(i):
        way, step = strip_way(i)
        return (z - step + NZ) % NZ if way == 0 else (z + step) % NZ

    turn(CAP // 2, CAP)
    inv_copy.wait()
    for what, *of in GATHER:
        if what == "y":
            c, d = of
            arrived(tall(origin(0, 0, d), c), gy_r.at[d * G_PIECES + c])
            for way in (0, 1):
                pass_on(c, way, 0, d)
        elif what == "z":
            c, way, step, d = of
            arrived(tall(origin(way, step + 1, d), c), gz_r.at[way, step, d * G_PIECES + c])
            if gather_has(way, step + 1, d):
                pass_on(c, way, step + 1, d)
        elif what == "b":
            way, step = of
            r = origin(way, step + 1, 0)
            arrived(short(r), hz_r.at[way, step])
            if short_has(way, step + 1):
                short_pass_on(way, step + 1)
            short_spread(short_at(way, step), r)
        elif what == "q":
            i, d = of
            arrived(short(origin(*strip_way(i), d)), hy_r.at[i, d])
        else:
            add_strip(strip_z(of[0]), of[0] == 0)

    far = (z + 4) % NZ
    for ours in (False, True):
        which = core if ours else 1 - core
        for g in (0, 1):
            ks = range(g * 4, g * 4 + 4)
            rows = [chip_at(k) * 2 + which for k in ks]
            out = jnp.dot(tile_rows(rows, far), strip(far), preferred_element_type=F32)
            for i, k in enumerate(ks):
                total = acc[rows[i]] + out[i * BS : (i + 1) * BS]
                if ours:
                    acc[rows[i]] = total
                else:
                    pair_out[k] = total.astype(BF)
            if not ours:
                group = pl.ds(g * 4, 4)
                send(pair_out.at[group], pair_in.at[group], pair_s.at[g], pair_r.at[g], sibling)
    for g in (0, 1):
        group = pl.ds(g * 4, 4)
        arrived(pair_in.at[group], pair_r.at[g])
        for k in range(g * 4, g * 4 + 4):
            total = acc[chip_at(k) * 2 + core] + pair_in[k].astype(F32)
            if k < CHIPS - 1:
                chip_out[k] = total.astype(BF)
                send(chip_out.at[k], chip_in.at[k], chip_s.at[k], chip_r.at[k], at_chip(k))
    for k in reversed(range(CHIPS - 1)):
        arrived(chip_in.at[k], chip_r.at[k])
        total = total + chip_in[k].astype(F32)

    for load in loads[5:]:
        load.wait()
    row_scale = down_rows(scale_of(deg[pl.ds(row * (CHIPS * 2) + col, 1), :]), F)
    propagated = (total * row_scale).astype(BF)
    pre = jnp.dot(propagated, weight[...], preferred_element_type=F32)
    square = pre * pre
    tanh = jnp.tanh(GELU_A * (pre + GELU_B * (square * pre)))
    cdf = 0.5 * (1.0 + tanh)
    slope = cdf + 0.5 * pre * (1.0 - tanh * tanh) * (GELU_A * (1.0 + 3.0 * GELU_B * square))
    pre_grad = (cot[...].astype(F32) * slope).astype(BF)
    back = lax.dot_general(
        pre_grad, weight[...], (((1,), (1,)), ((), ())), preferred_element_type=F32
    )
    grads[col] = (back * row_scale).astype(BF)

    mine = grads.at[col]
    for k in range(CHIPS - 1):
        send(mine, mine, ag_s.at[k], ag_r.at[k], at_chip(k))
    send(mine, mine, fw_s.at[CHIPS - 1], fw_r.at[CHIPS - 1], sibling)

    act_out[...] = (pre * cdf).astype(BF)
    w_local = lax.dot_general(
        propagated, pre_grad, (((0,), (0,)), ((), ())), preferred_element_type=F32
    )
    part[0] = w_local[0:BS]
    part[1] = w_local[BS:F]
    w_half_out[...] = part[1 - core].astype(BF)
    send(w_half_out, w_half_in, wh_s, wh_r, sibling)

    for k in reversed(range(CHIPS - 1)):
        ref = grads.at[chip_from(k) * 2 + core]
        arrived(ref, ag_r.at[k])
        send(ref, ref, fw_s.at[k], fw_r.at[k], sibling)

    arrived(w_half_in, wh_r)
    half = part[core] + w_half_in[...].astype(F32)
    for c in range(CHIPS):
        w_piece_out[c] = half[c * 16 : (c + 1) * 16].astype(BF)
    for k in range(CHIPS - 1):
        send(w_piece_out.at[chip_at(k)], w_piece_in.at[k], wp_s.at[k], wp_r.at[k], at_chip(k))

    for k in reversed(range(CHIPS)):
        arrived(grads.at[chip_from(k) * 2 + 1 - core], fw_r.at[k])

    def back_strip(i):
        way, step = strip_way(i)
        z_at = (z + step) % NZ if way == 0 else (z + NZ - step) % NZ
        lhs = jnp.concatenate(
            [
                jnp.concatenate(
                    [turned[lookup(r, ((y + d) % NY) * NZ + z_at)] for r in range(16)], axis=1
                )
                for d in range(NY)
            ],
            axis=0,
        )
        out = jnp.dot(lhs, grads[...].reshape(16 * BS, F), preferred_element_type=F32)
        part[pl.ds(i * NY, NY)] = out.reshape(NY, BS, F)

    def w_step(step):
        if step == 0:
            total = w_piece_out[chip].astype(F32)
            for k in range(CHIPS - 1):
                arrived(w_piece_in.at[k], wp_r.at[k])
                total = total + w_piece_in[k].astype(F32)
            w_z[z] = total.astype(BF)
            for k in range(1, NZ):
                send(w_z.at[z], w_z.at[z], wz_s.at[k], wz_r.at[k], at_z(k))
        if step == 1:
            for k in range(1, NZ):
                arrived(w_z.at[(z + NZ - k) % NZ], wz_r.at[k])
            total = w_z[0].astype(F32)
            for k in range(1, NZ):
                total = total + w_z[k].astype(F32)
            w_y[y] = total.astype(BF)
            for d in range(1, NY):
                send(w_y.at[y], w_y.at[y], wy_s.at[d], wy_r.at[d], at_y(d))
        if step == 2:
            for d in range(1, NY):
                arrived(w_y.at[(y + NY - d) % NY], wy_r.at[d])
            total = w_y[0].astype(F32)
            for d in range(1, NY):
                total = total + w_y[d].astype(F32)
            w_all[chip] = total.astype(BF)
            for k in range(CHIPS - 1):
                send(w_all.at[chip], w_all.at[chip], wa_s.at[k], wa_r.at[k], at_chip(k))
        if step == 3:
            for k in range(CHIPS - 1):
                arrived(w_all.at[chip_from(k)], wa_r.at[k])
            send(w_all, w_other, wo_s, wo_r, sibling)

    def short_total(i):
        total = part[i * NY, TALL:BS]
        for d in (1, 3, 2):
            arrived(short_in.at[i, d], ky_r.at[i, d])
            total = total + short_in[i, d].astype(F32)
        return total

    def rows_of(c):
        return slice(c * S_ROWS, (c + 1) * S_ROWS)

    def strip_at(way, step):
        return 4 - step if way == 0 or step == 0 else 8 - step

    for what, *of in SCATTER:
        if what == "c":
            back_strip(of[0])
        elif what == "q":
            i = of[0]
            for d in (2, 1, 3):
                short_out[i, d] = part[i * NY + d, TALL:BS].astype(BF)
                send(short_out.at[i, d], short_in.at[i, d], ky_s.at[i, d], ky_r.at[i, d], at_y(d))
        elif what == "z":
            c, way, step, d = of
            value = part[strip_at(way, step) * NY + d, rows_of(c)]
            rows, i = pl.ds(c * S_ROWS, S_ROWS), d * S_PIECES + c
            if step and scatter_has(way, step - 1, d):
                arrived(ring_in.at[way, step - 1, d, rows], rz_r.at[way, step - 1, i])
                value = value + ring_in[way, step - 1, d, rows_of(c)].astype(F32)
            ring_out[way, step, d, rows_of(c)] = value.astype(BF)
            send(
                ring_out.at[way, step, d, rows], ring_in.at[way, step, d, rows],
                rz_s.at[way, step, i], rz_r.at[way, step, i], at_z(1 if way == 0 else -1),
            )
        elif what == "b":
            way, step = of
            total = short_total(strip_at(way, step))
            if step and short_ring_has(way, step - 1):
                arrived(short_ring_in.at[way, step - 1], kz_r.at[way, step - 1])
                total = total + short_ring_in[way, step - 1].astype(F32)
            short_ring_out[way, step] = total.astype(BF)
            send(
                short_ring_out.at[way, step], short_ring_in.at[way, step],
                kz_s.at[way, step], kz_r.at[way, step], at_z(1 if way == 0 else -1),
            )
        elif what == "w":
            w_step(of[0])
        elif what == "s":
            total = short_total(0)
            for way in (0, 1):
                arrived(short_ring_in.at[way, 3], kz_r.at[way, 3])
                total = total + short_ring_in[way, 3].astype(F32)
            fg_out[TALL:BS, :] = (total * own_scale[TALL:BS]).astype(BF)
        else:
            c, d = of[0], of[1] if what == "y" else 0
            rows, i = pl.ds(c * S_ROWS, S_ROWS), d * S_PIECES + c
            value = part[d, rows_of(c)]
            for way in (0, 1):
                arrived(ring_in.at[way, 3, d, rows], rz_r.at[way, 3, i])
                value = value + ring_in[way, 3, d, rows_of(c)].astype(F32)
            if what == "y":
                last_out[d, rows_of(c)] = value.astype(BF)
                send(last_out.at[d, rows], last_in.at[d, rows], ry_s.at[i], ry_r.at[i], at_y(d))
                continue
            for d in (1, 3, 2):
                arrived(last_in.at[d, rows], ry_r.at[d * S_PIECES + c])
                value = value + last_in[d, rows_of(c)].astype(F32)
            fg_out[rows_of(c), :] = (value * own_scale[rows_of(c)]).astype(BF)

    arrived(w_other, wo_r)
    wg_out[pl.ds(pl.multiple_of(core * BS, BS), BS), :] = w_all[...].astype(F32).reshape(BS, F)
    wg_out[pl.ds(pl.multiple_of((1 - core) * BS, BS), BS), :] = (
        w_other[...].astype(F32).reshape(BS, F)
    )

    for copy in started:
        copy.wait_send()


def per_device(
    features, weight, cotangent, degrees, adj_blocks, block_rows, block_cols, block_count
):
    vmem = pl.BlockSpec(memory_space=pltpu.VMEM)
    dma = pltpu.SemaphoreType.DMA
    block = (BS, F)
    high, low = (TALL, F), (BS - TALL, F)
    scratch = [
        pltpu.VMEM(block, BF),
        pltpu.VMEM((F, F), BF),
        pltpu.VMEM(block, BF),
        pltpu.VMEM((512, BS), I32),
        pltpu.VMEM((1, BS), I32),
        pltpu.VMEM((1, BS), I32),
        pltpu.SMEM((1, 1), I32),
        pltpu.VMEM((CAP + 1, BS, BS), BF),
        pltpu.VMEM((CAP + 1, BS, BS), BF),
        pltpu.VMEM((NY * NZ,) + block, BF),
        pltpu.VMEM((CHIPS * 2,) + block, F32),
        pltpu.VMEM((8, BS), I32),
        pltpu.SMEM((8, BS), I32),
        pltpu.VMEM((CHIPS,) + block, BF),
        pltpu.VMEM((CHIPS,) + block, BF),
        pltpu.VMEM((CHIPS,) + block, BF),
        pltpu.VMEM((CHIPS,) + block, BF),
        pltpu.VMEM((CHIPS * 2,) + block, BF),
        pltpu.VMEM((NZ * NY,) + block, F32),
        pltpu.VMEM((2, 4, NY) + high, BF),
        pltpu.VMEM((2, 4, NY) + high, BF),
        pltpu.VMEM((NY,) + high, BF),
        pltpu.VMEM((NY,) + high, BF),
        pltpu.VMEM(block, BF),
        pltpu.VMEM(block, BF),
        pltpu.VMEM((CHIPS, 16, F), BF),
        pltpu.VMEM((CHIPS, 16, F), BF),
        pltpu.VMEM((NZ, 16, F), BF),
        pltpu.VMEM((NY, 16, F), BF),
        pltpu.VMEM((CHIPS, 16, F), BF),
        pltpu.VMEM((CHIPS, 16, F), BF),
        pltpu.VMEM((NZ, NY) + low, BF),
        pltpu.VMEM((NZ, NY) + low, BF),
        pltpu.VMEM((2, 4) + low, BF),
        pltpu.VMEM((2, 4) + low, BF),
    ]
    sems = [dma((7,)), dma, dma]
    for shape in (
        (NY * G_PIECES,), (2, 4, NY * G_PIECES), (2,), (CHIPS,), (CHIPS,), (CHIPS,),
        (2, 4, NY * S_PIECES), (NY * S_PIECES,),
        None, (CHIPS,), (NZ,), (NY,), (CHIPS,), None,
        (2, 4), (NZ, NY), (2, 4), (NZ, NY),
    ):
        sems += [dma if shape is None else dma(shape)] * 2
    return pl.pallas_call(
        kernel,
        out_shape=(
            jax.ShapeDtypeStruct(block, BF),
            jax.ShapeDtypeStruct(block, BF),
            jax.ShapeDtypeStruct((F, F), F32),
        ),
        in_specs=[pl.BlockSpec(memory_space=pltpu.HBM)] * 8,
        out_specs=(vmem, vmem, vmem),
        scratch_shapes=scratch + sems,
        compiler_params=pltpu.CompilerParams(
            collective_id=0, has_side_effects=True, vmem_limit_bytes=58 * 1024 * 1024
        ),
        cost_estimate=pl.CostEstimate(
            flops=8 * 2048 * 4096 * 256 // 2, bytes_accessed=5 * 1024 * 1024, transcendentals=32768
        ),
        name="layer",
    )(
        features,
        weight,
        cotangent,
        degrees.reshape(-1, BS),
        adj_blocks.reshape(CAP, BS, BS),
        block_rows.reshape(1, CAP),
        block_cols.reshape(1, CAP),
        block_count,
    )


def solution(mesh):
    in_specs = (
        P(("col", "row"), None),
        P(),
        P(("row", "col"), None),
        P(),
        P("row", "col", None, None, None),
        P("row", "col", None),
        P("row", "col", None),
        P("row", "col"),
    )
    out_specs = (P(("row", "col"), None), P(("col", "row"), None), P())
    return jax.shard_map(
        per_device, mesh=mesh, in_specs=in_specs, out_specs=out_specs, check_vma=False
    )
```

```python
import math

import jax
import jax.numpy as jnp
from jax import lax
from jax.experimental import pallas as pl
from jax.experimental.pallas import tpu as pltpu
from jax.sharding import PartitionSpec as P

NY, NZ = 4, 8
NX, NL = 4, 2
CHIPS = NX * NL
BS = 128
F = 256
CAP = 128
BF, F32, I32 = jnp.bfloat16, jnp.float32, jnp.int32
MESH = pl.DeviceIdType.MESH

GELU_A = math.sqrt(2.0 / math.pi)
GELU_B = 0.044715

TALL = 96
G_PIECES, S_PIECES = 1, 1
G_ROWS, S_ROWS = TALL // G_PIECES, TALL // S_PIECES
GATHER = (
    ("z", 0, 0, 0, 0), ("z", 0, 1, 0, 0), ("b", 0, 0), ("b", 1, 0), ("y", 0, 1), ("y", 0, 3),
    ("z", 0, 0, 1, 0), ("z", 0, 1, 1, 0), ("b", 0, 1), ("b", 1, 1), ("z", 0, 0, 0, 1), ("y", 0, 2),
    ("z", 0, 1, 0, 1), ("q", 0, 1), ("q", 0, 3), ("q", 0, 2), ("c", 0), ("z", 0, 0, 0, 3),
    ("z", 0, 1, 0, 3), ("q", 1, 1), ("q", 1, 3), ("z", 0, 0, 2, 0), ("q", 1, 2), ("z", 0, 1, 2, 0),
    ("b", 0, 2), ("b", 1, 2), ("q", 5, 1), ("q", 5, 3), ("z", 0, 0, 1, 1), ("q", 5, 2),
    ("z", 0, 1, 0, 2), ("c", 5), ("z", 0, 0, 0, 2), ("q", 2, 1), ("c", 1), ("q", 2, 3),
    ("z", 0, 1, 1, 1), ("q", 2, 2), ("z", 0, 0, 1, 3), ("z", 0, 1, 1, 3), ("q", 6, 1), ("q", 6, 3),
    ("q", 6, 2), ("z", 0, 0, 3, 0), ("z", 0, 1, 1, 2), ("c", 6), ("b", 0, 3), ("q", 3, 1),
    ("q", 3, 3), ("q", 3, 2), ("z", 0, 0, 2, 1), ("z", 0, 1, 2, 1), ("q", 7, 1), ("q", 7, 3),
    ("z", 0, 0, 1, 2), ("q", 7, 2), ("c", 2), ("z", 0, 1, 2, 3), ("z", 0, 0, 2, 3),
    ("z", 0, 1, 2, 2), ("c", 7), ("z", 0, 0, 3, 1), ("q", 4, 1), ("q", 4, 3), ("q", 4, 2),
    ("z", 0, 0, 2, 2), ("c", 3), ("z", 0, 1, 3, 3), ("z", 0, 1, 3, 2),
)
SCATTER = (
    ("c", 4), ("z", 0, 0, 0, 2), ("z", 0, 1, 0, 1), ("z", 0, 1, 0, 3), ("z", 0, 0, 0, 0), ("q", 4),
    ("c", 3), ("z", 0, 0, 1, 1), ("z", 0, 0, 1, 3), ("q", 3), ("c", 7), ("z", 0, 1, 1, 2),
    ("z", 0, 1, 1, 0), ("q", 7), ("z", 0, 0, 1, 2), ("z", 0, 1, 1, 1), ("c", 2), ("q", 2), ("w", 0),
    ("z", 0, 1, 1, 3), ("z", 0, 0, 1, 0), ("c", 6), ("b", 0, 0), ("z", 0, 0, 2, 1), ("q", 6),
    ("z", 0, 1, 2, 2), ("c", 1), ("z", 0, 0, 2, 3), ("q", 1), ("z", 0, 1, 2, 0), ("c", 5),
    ("z", 0, 0, 2, 2), ("w", 1), ("q", 5), ("b", 1, 1), ("z", 0, 1, 2, 1), ("z", 0, 0, 2, 0),
    ("c", 0), ("b", 0, 1), ("z", 0, 1, 2, 3), ("q", 0), ("z", 0, 0, 3, 1), ("z", 0, 1, 3, 2),
    ("z", 0, 0, 3, 3), ("z", 0, 1, 3, 0), ("w", 2), ("b", 1, 2), ("z", 0, 0, 3, 2),
    ("z", 0, 1, 3, 1), ("z", 0, 0, 3, 0), ("b", 0, 2), ("z", 0, 1, 3, 3), ("w", 3), ("b", 1, 3),
    ("y", 0, 2), ("y", 0, 1), ("b", 0, 3), ("y", 0, 3), ("s",), ("t", 0),
)
CHIP_ORDER = ((1, 2), (1, 1), (1, 3), (1, 0), (0, 2), (0, 1), (0, 3), (0, 0))


def scale_of(degrees):
    safe = jnp.maximum(degrees, 1).astype(F32)
    return jnp.where(degrees > 0, lax.rsqrt(safe), jnp.float32(0.0))


def down_rows(line, width):
    square = jnp.broadcast_to(line, (BS, BS)).T
    return jnp.concatenate([square] * (width // BS), axis=1) if width > BS else square


def short_has(way, step):
    return step < 3 or (step == 3 and way == 0)


def short_at(way, step):
    return 1 + step + 4 * way


def gather_has(way, step, d):
    return step < 3 or (step == 3 and (d in (0, 1)) == (way == 0))


def short_ring_has(way, step):
    return step > 0 or way == 0


def scatter_has(way, step, d):
    return step > 0 or (d in (2, 0)) == (way == 0)


def kernel(
    feat_h, weight_h, cot_h, deg_h, adj, brow_h, bcol_h, cnt_h,
    act_out, fg_out, wg_out,
    feat, weight, cot, deg, brow, bcol, cnt,
    blocks, turned, src, acc, inv_v, inv_s,
    pair_out, pair_in, chip_out, chip_in, grads,
    part, ring_out, ring_in, last_out, last_in,
    w_half_out, w_half_in, w_piece_out, w_piece_in, w_z, w_y, w_all, w_other,
    short_out, short_in, short_ring_out, short_ring_in,
    in_sem, adj_sem, inv_sem, gy_s, gy_r, gz_s, gz_r, pair_s, pair_r, chip_s, chip_r,
    ag_s, ag_r, fw_s, fw_r, rz_s, rz_r, ry_s, ry_r,
    wh_s, wh_r, wp_s, wp_r, wz_s, wz_r, wy_s, wy_r, wa_s, wa_r, wo_s, wo_r,
    hz_s, hz_r, hy_s, hy_r, kz_s, kz_r, ky_s, ky_r,
):
    row = lax.axis_index("row")
    col = lax.axis_index("col")
    y, z = row // NZ, row % NZ
    chip, core = col // 2, col % 2
    ylo, x = chip // NX, chip % NX

    def at_z(k):
        return (y * NZ + (z + k + NZ) % NZ, col)

    def at_y(d):
        return (((y + d) % NY) * NZ + z, col)

    def chip_at(k):
        dl, dx = CHIP_ORDER[k]
        return ((ylo + dl) % NL) * NX + (x + dx) % NX

    def chip_from(k):
        dl, dx = CHIP_ORDER[k]
        return ((ylo + NL - dl) % NL) * NX + (x + NX - dx) % NX

    def at_chip(k):
        return (row, chip_at(k) * 2 + core)

    sibling = (row, chip * 2 + 1 - core)

    loads = [
        pltpu.make_async_copy(source, target, in_sem.at[i])
        for i, (source, target) in enumerate(
            (
                (deg_h, deg), (feat_h, feat), (brow_h, brow), (bcol_h, bcol),
                (cnt_h, cnt), (weight_h, weight), (cot_h, cot),
            )
        )
    ]
    for load in loads:
        load.start()
    adj_copy = pltpu.make_async_copy(adj, blocks.at[pl.ds(0, CAP)], adj_sem)
    adj_copy.start()

    barrier = pltpu.get_barrier_semaphore()
    partners = [at_z(k) for k in range(1, NZ)] + [at_y(d) for d in range(1, NY)]
    partners += [at_chip(k) for k in range(CHIPS - 1)] + [sibling]
    for partner in partners:
        pl.semaphore_signal(barrier, inc=1, device_id=partner, device_id_type=MESH)

    for load in loads[:2]:
        load.wait()
    own_scale = down_rows(scale_of(deg[pl.ds(col * (NY * NZ) + row, 1), :]), F)
    src[row] = (feat[...].astype(F32) * own_scale).astype(BF)

    pl.semaphore_wait(barrier, len(partners))

    started = []

    def send(source, target, send_sem, recv_sem, device):
        copy = pltpu.make_async_remote_copy(
            src_ref=source, dst_ref=target, send_sem=send_sem, recv_sem=recv_sem,
            device_id=device, device_id_type=MESH,
        )
        copy.start()
        started.append(copy)

    def arrived(buffer, recv_sem):
        pltpu.make_async_remote_copy(
            src_ref=buffer, dst_ref=buffer, send_sem=recv_sem, recv_sem=recv_sem,
            device_id=sibling, device_id_type=MESH,
        ).wait_recv()

    def origin(way, step, d):
        zz = (z - step + NZ) % NZ if way == 0 else (z + step) % NZ
        return ((y + NY - d) % NY) * NZ + zz

    def tall(r, c):
        return src.at[r, pl.ds(c * G_ROWS, G_ROWS)]

    def short(r):
        return src.at[r, pl.ds(TALL, BS - TALL)]

    def pass_on(c, way, step, d):
        ref = tall(origin(way, step, d), c)
        i = d * G_PIECES + c
        send(ref, ref, gz_s.at[way, step, i], gz_r.at[way, step, i], at_z(1 if way == 0 else -1))

    def short_pass_on(way, step):
        ref = short(origin(way, step, 0))
        send(ref, ref, hz_s.at[way, step], hz_r.at[way, step], at_z(1 if way == 0 else -1))

    def short_spread(i, r):
        for d in (2, 1, 3):
            send(short(r), short(r), hy_s.at[i, d], hy_r.at[i, d], at_y(d))

    for c in range(G_PIECES):
        for way in (0, 1):
            pass_on(c, way, 0, 0)
    for c in range(G_PIECES):
        for d in (1, 3, 2):
            i = d * G_PIECES + c
            send(tall(row, c), tall(row, c), gy_s.at[i], gy_r.at[i], at_y(d))
    for way in (0, 1):
        short_pass_on(way, 0)
    short_spread(0, row)

    for load in loads[2:5]:
        load.wait()
    lane = lax.broadcasted_iota(I32, (1, BS), 1)
    place = jnp.where(lane < cnt[0, 0], brow[...] * 32 + bcol[...], -1)
    place = jnp.broadcast_to(place, (BS, BS)).T
    slot = lax.broadcasted_iota(I32, (BS, BS), 0)
    spot = lax.broadcasted_iota(I32, (BS, BS), 1)
    for q in range(4):
        hit = jnp.where(place == spot + q * BS, slot - CAP, 0)
        inv_v[q : q + 1, :] = jnp.sum(hit, axis=0, keepdims=True) + CAP
    inv_v[4:8, :] = jnp.zeros((4, BS), I32)
    inv_copy = pltpu.make_async_copy(inv_v, inv_s, inv_sem)
    inv_copy.start()
    blocks[CAP] = jnp.zeros((BS, BS), BF)
    turned[CAP] = jnp.zeros((BS, BS), BF)

    def turn(first, last):
        def one(k, carry):
            turned[k] = blocks[k].T
            return carry

        lax.fori_loop(first, last, one, 0)

    def lookup(r, c):
        return inv_s[r // 4, (r % 4) * 32 + c]

    def strip(z_at):
        return jnp.concatenate([src[yy * NZ + z_at] for yy in range(NY)], axis=0)

    def tile_rows(rows, z_at):
        return jnp.concatenate(
            [
                jnp.concatenate([blocks[lookup(r, yy * NZ + z_at)] for yy in range(NY)], axis=1)
                for r in rows
            ],
            axis=0,
        )

    def add_strip(z_at, first):
        def some(g, carry):
            out = jnp.dot(
                tile_rows([g * 4 + i for i in range(4)], z_at), strip(z_at),
                preferred_element_type=F32,
            ).reshape(4, BS, F)
            if first:
                acc[pl.ds(g * 4, 4)] = out
            else:
                acc[pl.ds(g * 4, 4)] += out
            return carry

        lax.fori_loop(0, 4, some, 0)

    def strip_way(i):
        return (0, i) if i <= 4 else (1, i - 4)

    def strip_z(i):
        way, step = strip_way(i)
        return (z - step + NZ) % NZ if way == 0 else (z + step) % NZ

    adj_copy.wait()
    turn(0, CAP)
    inv_copy.wait()
    for what, *of in GATHER:
        if what == "y":
            c, d = of
            arrived(tall(origin(0, 0, d), c), gy_r.at[d * G_PIECES + c])
            for way in (0, 1):
                pass_on(c, way, 0, d)
        elif what == "z":
            c, way, step, d = of
            arrived(tall(origin(way, step + 1, d), c), gz_r.at[way, step, d * G_PIECES + c])
            if gather_has(way, step + 1, d):
                pass_on(c, way, step + 1, d)
        elif what == "b":
            way, step = of
            r = origin(way, step + 1, 0)
            arrived(short(r), hz_r.at[way, step])
            if short_has(way, step + 1):
                short_pass_on(way, step + 1)
            short_spread(short_at(way, step), r)
        elif what == "q":
            i, d = of
            arrived(short(origin(*strip_way(i), d)), hy_r.at[i, d])
        else:
            add_strip(strip_z(of[0]), of[0] == 0)

    far = (z + 4) % NZ
    for ours in (False, True):
        which = core if ours else 1 - core
        for g in (0, 1):
            ks = range(g * 4, g * 4 + 4)
            rows = [chip_at(k) * 2 + which for k in ks]
            out = jnp.dot(tile_rows(rows, far), strip(far), preferred_element_type=F32)
            for i, k in enumerate(ks):
                total = acc[rows[i]] + out[i * BS : (i + 1) * BS]
                if ours:
                    acc[rows[i]] = total
                else:
                    pair_out[k] = total.astype(BF)
            if not ours:
                group = pl.ds(g * 4, 4)
                send(pair_out.at[group], pair_in.at[group], pair_s.at[g], pair_r.at[g], sibling)
    for g in (0, 1):
        group = pl.ds(g * 4, 4)
        arrived(pair_in.at[group], pair_r.at[g])
        for k in range(g * 4, g * 4 + 4):
            total = acc[chip_at(k) * 2 + core] + pair_in[k].astype(F32)
            if k < CHIPS - 1:
                chip_out[k] = total.astype(BF)
                send(chip_out.at[k], chip_in.at[k], chip_s.at[k], chip_r.at[k], at_chip(k))
    for k in reversed(range(CHIPS - 1)):
        arrived(chip_in.at[k], chip_r.at[k])
        total = total + chip_in[k].astype(F32)

    for load in loads[5:]:
        load.wait()
    row_scale = down_rows(scale_of(deg[pl.ds(row * (CHIPS * 2) + col, 1), :]), F)
    propagated = (total * row_scale).astype(BF)
    pre = jnp.dot(propagated, weight[...], preferred_element_type=F32)
    square = pre * pre
    tanh = jnp.tanh(GELU_A * (pre + GELU_B * (square * pre)))
    cdf = 0.5 * (1.0 + tanh)
    slope = cdf + 0.5 * pre * (1.0 - tanh * tanh) * (GELU_A * (1.0 + 3.0 * GELU_B * square))
    pre_grad = (cot[...].astype(F32) * slope).astype(BF)
    back = lax.dot_general(
        pre_grad, weight[...], (((1,), (1,)), ((), ())), preferred_element_type=F32
    )
    grads[col] = (back * row_scale).astype(BF)

    mine = grads.at[col]
    for k in range(CHIPS - 1):
        send(mine, mine, ag_s.at[k], ag_r.at[k], at_chip(k))
    send(mine, mine, fw_s.at[CHIPS - 1], fw_r.at[CHIPS - 1], sibling)

    act_out[...] = (pre * cdf).astype(BF)
    w_local = lax.dot_general(
        propagated, pre_grad, (((0,), (0,)), ((), ())), preferred_element_type=F32
    )
    part[0] = w_local[0:BS]
    part[1] = w_local[BS:F]
    w_half_out[...] = part[1 - core].astype(BF)
    send(w_half_out, w_half_in, wh_s, wh_r, sibling)

    for k in reversed(range(CHIPS - 1)):
        ref = grads.at[chip_from(k) * 2 + core]
        arrived(ref, ag_r.at[k])
        send(ref, ref, fw_s.at[k], fw_r.at[k], sibling)

    arrived(w_half_in, wh_r)
    half = part[core] + w_half_in[...].astype(F32)
    for c in range(CHIPS):
        w_piece_out[c] = half[c * 16 : (c + 1) * 16].astype(BF)
    for k in range(CHIPS - 1):
        send(w_piece_out.at[chip_at(k)], w_piece_in.at[k], wp_s.at[k], wp_r.at[k], at_chip(k))

    for k in reversed(range(CHIPS)):
        arrived(grads.at[chip_from(k) * 2 + 1 - core], fw_r.at[k])

    def back_strip(i):
        way, step = strip_way(i)
        z_at = (z + step) % NZ if way == 0 else (z + NZ - step) % NZ
        lhs = jnp.concatenate(
            [
                jnp.concatenate(
                    [turned[lookup(r, ((y + d) % NY) * NZ + z_at)] for r in range(16)], axis=1
                )
                for d in range(NY)
            ],
            axis=0,
        )
        out = jnp.dot(lhs, grads[...].reshape(16 * BS, F), preferred_element_type=F32)
        part[pl.ds(i * NY, NY)] = out.reshape(NY, BS, F)

    def w_step(step):
        if step == 0:
            total = w_piece_out[chip].astype(F32)
            for k in range(CHIPS - 1):
                arrived(w_piece_in.at[k], wp_r.at[k])
                total = total + w_piece_in[k].astype(F32)
            w_z[z] = total.astype(BF)
            for k in range(1, NZ):
                send(w_z.at[z], w_z.at[z], wz_s.at[k], wz_r.at[k], at_z(k))
        if step == 1:
            for k in range(1, NZ):
                arrived(w_z.at[(z + NZ - k) % NZ], wz_r.at[k])
            total = w_z[0].astype(F32)
            for k in range(1, NZ):
                total = total + w_z[k].astype(F32)
            w_y[y] = total.astype(BF)
            for d in range(1, NY):
                send(w_y.at[y], w_y.at[y], wy_s.at[d], wy_r.at[d], at_y(d))
        if step == 2:
            for d in range(1, NY):
                arrived(w_y.at[(y + NY - d) % NY], wy_r.at[d])
            total = w_y[0].astype(F32)
            for d in range(1, NY):
                total = total + w_y[d].astype(F32)
            w_all[chip] = total.astype(BF)
            for k in range(CHIPS - 1):
                send(w_all.at[chip], w_all.at[chip], wa_s.at[k], wa_r.at[k], at_chip(k))
        if step == 3:
            for k in range(CHIPS - 1):
                arrived(w_all.at[chip_from(k)], wa_r.at[k])
            send(w_all, w_other, wo_s, wo_r, sibling)

    def short_total(i):
        total = part[i * NY, TALL:BS]
        for d in (1, 3, 2):
            arrived(short_in.at[i, d], ky_r.at[i, d])
            total = total + short_in[i, d].astype(F32)
        return total

    def rows_of(c):
        return slice(c * S_ROWS, (c + 1) * S_ROWS)

    def strip_at(way, step):
        return 4 - step if way == 0 or step == 0 else 8 - step

    for what, *of in SCATTER:
        if what == "c":
            back_strip(of[0])
        elif what == "q":
            i = of[0]
            for d in (2, 1, 3):
                short_out[i, d] = part[i * NY + d, TALL:BS].astype(BF)
                send(short_out.at[i, d], short_in.at[i, d], ky_s.at[i, d], ky_r.at[i, d], at_y(d))
        elif what == "z":
            c, way, step, d = of
            value = part[strip_at(way, step) * NY + d, rows_of(c)]
            rows, i = pl.ds(c * S_ROWS, S_ROWS), d * S_PIECES + c
            if step and scatter_has(way, step - 1, d):
                arrived(ring_in.at[way, step - 1, d, rows], rz_r.at[way, step - 1, i])
                value = value + ring_in[way, step - 1, d, rows_of(c)].astype(F32)
            ring_out[way, step, d, rows_of(c)] = value.astype(BF)
            send(
                ring_out.at[way, step, d, rows], ring_in.at[way, step, d, rows],
                rz_s.at[way, step, i], rz_r.at[way, step, i], at_z(1 if way == 0 else -1),
            )
        elif what == "b":
            way, step = of
            total = short_total(strip_at(way, step))
            if step and short_ring_has(way, step - 1):
                arrived(short_ring_in.at[way, step - 1], kz_r.at[way, step - 1])
                total = total + short_ring_in[way, step - 1].astype(F32)
            short_ring_out[way, step] = total.astype(BF)
            send(
                short_ring_out.at[way, step], short_ring_in.at[way, step],
                kz_s.at[way, step], kz_r.at[way, step], at_z(1 if way == 0 else -1),
            )
        elif what == "w":
            w_step(of[0])
        elif what == "s":
            total = short_total(0)
            for way in (0, 1):
                arrived(short_ring_in.at[way, 3], kz_r.at[way, 3])
                total = total + short_ring_in[way, 3].astype(F32)
            fg_out[TALL:BS, :] = (total * own_scale[TALL:BS]).astype(BF)
        else:
            c, d = of[0], of[1] if what == "y" else 0
            rows, i = pl.ds(c * S_ROWS, S_ROWS), d * S_PIECES + c
            value = part[d, rows_of(c)]
            for way in (0, 1):
                arrived(ring_in.at[way, 3, d, rows], rz_r.at[way, 3, i])
                value = value + ring_in[way, 3, d, rows_of(c)].astype(F32)
            if what == "y":
                last_out[d, rows_of(c)] = value.astype(BF)
                send(last_out.at[d, rows], last_in.at[d, rows], ry_s.at[i], ry_r.at[i], at_y(d))
                continue
            for d in (1, 3, 2):
                arrived(last_in.at[d, rows], ry_r.at[d * S_PIECES + c])
                value = value + last_in[d, rows_of(c)].astype(F32)
            fg_out[rows_of(c), :] = (value * own_scale[rows_of(c)]).astype(BF)

    arrived(w_other, wo_r)
    wg_out[pl.ds(pl.multiple_of(core * BS, BS), BS), :] = w_all[...].astype(F32).reshape(BS, F)
    wg_out[pl.ds(pl.multiple_of((1 - core) * BS, BS), BS), :] = (
        w_other[...].astype(F32).reshape(BS, F)
    )

    for copy in started:
        copy.wait_send()


def per_device(
    features, weight, cotangent, degrees, adj_blocks, block_rows, block_cols, block_count
):
    vmem = pl.BlockSpec(memory_space=pltpu.VMEM)
    dma = pltpu.SemaphoreType.DMA
    block = (BS, F)
    high, low = (TALL, F), (BS - TALL, F)
    scratch = [
        pltpu.VMEM(block, BF),
        pltpu.VMEM((F, F), BF),
        pltpu.VMEM(block, BF),
        pltpu.VMEM((512, BS), I32),
        pltpu.VMEM((1, BS), I32),
        pltpu.VMEM((1, BS), I32),
        pltpu.SMEM((1, 1), I32),
        pltpu.VMEM((CAP + 1, BS, BS), BF),
        pltpu.VMEM((CAP + 1, BS, BS), BF),
        pltpu.VMEM((NY * NZ,) + block, BF),
        pltpu.VMEM((CHIPS * 2,) + block, F32),
        pltpu.VMEM((8, BS), I32),
        pltpu.SMEM((8, BS), I32),
        pltpu.VMEM((CHIPS,) + block, BF),
        pltpu.VMEM((CHIPS,) + block, BF),
        pltpu.VMEM((CHIPS,) + block, BF),
        pltpu.VMEM((CHIPS,) + block, BF),
        pltpu.VMEM((CHIPS * 2,) + block, BF),
        pltpu.VMEM((NZ * NY,) + block, F32),
        pltpu.VMEM((2, 4, NY) + high, BF),
        pltpu.VMEM((2, 4, NY) + high, BF),
        pltpu.VMEM((NY,) + high, BF),
        pltpu.VMEM((NY,) + high, BF),
        pltpu.VMEM(block, BF),
        pltpu.VMEM(block, BF),
        pltpu.VMEM((CHIPS, 16, F), BF),
        pltpu.VMEM((CHIPS, 16, F), BF),
        pltpu.VMEM((NZ, 16, F), BF),
        pltpu.VMEM((NY, 16, F), BF),
        pltpu.VMEM((CHIPS, 16, F), BF),
        pltpu.VMEM((CHIPS, 16, F), BF),
        pltpu.VMEM((NZ, NY) + low, BF),
        pltpu.VMEM((NZ, NY) + low, BF),
        pltpu.VMEM((2, 4) + low, BF),
        pltpu.VMEM((2, 4) + low, BF),
    ]
    sems = [dma((7,)), dma, dma]
    for shape in (
        (NY * G_PIECES,), (2, 4, NY * G_PIECES), (2,), (CHIPS,), (CHIPS,), (CHIPS,),
        (2, 4, NY * S_PIECES), (NY * S_PIECES,),
        None, (CHIPS,), (NZ,), (NY,), (CHIPS,), None,
        (2, 4), (NZ, NY), (2, 4), (NZ, NY),
    ):
        sems += [dma if shape is None else dma(shape)] * 2
    return pl.pallas_call(
        kernel,
        out_shape=(
            pltpu.VMEM(block, BF),
            pltpu.VMEM(block, BF),
            pltpu.VMEM((F, F), F32),
        ),
        in_specs=[pl.BlockSpec(memory_space=pltpu.HBM)] * 8,
        out_specs=(vmem, vmem, vmem),
        scratch_shapes=scratch + sems,
        compiler_params=pltpu.CompilerParams(
            collective_id=0, has_side_effects=True, vmem_limit_bytes=58 * 1024 * 1024
        ),
        cost_estimate=pl.CostEstimate(
            flops=8 * 2048 * 4096 * 256 // 2, bytes_accessed=5 * 1024 * 1024, transcendentals=32768
        ),
        name="layer",
    )(
        features,
        weight,
        cotangent,
        degrees.reshape(-1, BS),
        adj_blocks.reshape(CAP, BS, BS),
        block_rows.reshape(1, CAP),
        block_cols.reshape(1, CAP),
        block_count,
    )


def solution(mesh):
    in_specs = (
        P(("col", "row"), None),
        P(),
        P(("row", "col"), None),
        P(),
        P("row", "col", None, None, None),
        P("row", "col", None),
        P("row", "col", None),
        P("row", "col"),
    )
    out_specs = (P(("row", "col"), None), P(("col", "row"), None), P())
    return jax.shard_map(
        per_device, mesh=mesh, in_specs=in_specs, out_specs=out_specs, check_vma=False
    )
```

```python
import math

import jax
import jax.numpy as jnp
from jax import lax
from jax.experimental import pallas as pl
from jax.experimental.pallas import tpu as pltpu
from jax.sharding import PartitionSpec as P

NY, NZ = 4, 8
NX, NL = 4, 2
CHIPS = NX * NL
BS = 128
F = 256
CAP = 128
BF, F32, I32 = jnp.bfloat16, jnp.float32, jnp.int32
MESH = pl.DeviceIdType.MESH

GELU_A = math.sqrt(2.0 / math.pi)
GELU_B = 0.044715

TALL = 96
G_PIECES, S_PIECES = 1, 1
G_ROWS, S_ROWS = TALL // G_PIECES, TALL // S_PIECES
GATHER = (
    ("z", 0, 0, 0, 0), ("z", 0, 1, 0, 0), ("b", 0, 0), ("b", 1, 0), ("y", 0, 1), ("y", 0, 3),
    ("z", 0, 0, 1, 0), ("z", 0, 1, 1, 0), ("b", 0, 1), ("b", 1, 1), ("z", 0, 0, 0, 1), ("y", 0, 2),
    ("z", 0, 1, 0, 1), ("q", 0, 1), ("q", 0, 3), ("q", 0, 2), ("c", 0), ("z", 0, 0, 0, 3),
    ("z", 0, 1, 0, 3), ("q", 1, 1), ("q", 1, 3), ("z", 0, 0, 2, 0), ("q", 1, 2), ("z", 0, 1, 2, 0),
    ("b", 0, 2), ("b", 1, 2), ("q", 5, 1), ("q", 5, 3), ("z", 0, 0, 1, 1), ("q", 5, 2),
    ("z", 0, 1, 0, 2), ("c", 5), ("z", 0, 0, 0, 2), ("q", 2, 1), ("c", 1), ("q", 2, 3),
    ("z", 0, 1, 1, 1), ("q", 2, 2), ("z", 0, 0, 1, 3), ("z", 0, 1, 1, 3), ("q", 6, 1), ("q", 6, 3),
    ("q", 6, 2), ("z", 0, 0, 3, 0), ("z", 0, 1, 1, 2), ("c", 6), ("b", 0, 3), ("q", 3, 1),
    ("q", 3, 3), ("q", 3, 2), ("z", 0, 0, 2, 1), ("z", 0, 1, 2, 1), ("q", 7, 1), ("q", 7, 3),
    ("z", 0, 0, 1, 2), ("q", 7, 2), ("c", 2), ("z", 0, 1, 2, 3), ("z", 0, 0, 2, 3),
    ("z", 0, 1, 2, 2), ("c", 7), ("z", 0, 0, 3, 1), ("q", 4, 1), ("q", 4, 3), ("q", 4, 2),
    ("z", 0, 0, 2, 2), ("c", 3), ("z", 0, 1, 3, 3), ("z", 0, 1, 3, 2),
)
SCATTER = (
    ("d", 4, 2, 1), ("z", 0, 0, 0, 2), ("z", 0, 1, 0, 1), ("d", 4, 3, 0), ("z", 0, 1, 0, 3),
    ("z", 0, 0, 0, 0), ("q", 4), ("c", 3), ("z", 0, 0, 1, 1), ("z", 0, 0, 1, 3), ("q", 3), ("c", 7),
    ("z", 0, 1, 1, 2), ("z", 0, 1, 1, 0), ("q", 7), ("z", 0, 0, 1, 2), ("z", 0, 1, 1, 1), ("c", 2),
    ("q", 2), ("w", 0), ("z", 0, 1, 1, 3), ("z", 0, 0, 1, 0), ("c", 6), ("b", 0, 0),
    ("z", 0, 0, 2, 1), ("q", 6), ("z", 0, 1, 2, 2), ("c", 1), ("z", 0, 0, 2, 3), ("q", 1),
    ("z", 0, 1, 2, 0), ("c", 5), ("z", 0, 0, 2, 2), ("w", 1), ("q", 5), ("b", 1, 1),
    ("z", 0, 1, 2, 1), ("z", 0, 0, 2, 0), ("c", 0), ("b", 0, 1), ("z", 0, 1, 2, 3), ("q", 0),
    ("z", 0, 0, 3, 1), ("z", 0, 1, 3, 2), ("z", 0, 0, 3, 3), ("z", 0, 1, 3, 0), ("w", 2),
    ("b", 1, 2), ("z", 0, 0, 3, 2), ("z", 0, 1, 3, 1), ("z", 0, 0, 3, 0), ("b", 0, 2),
    ("z", 0, 1, 3, 3), ("w", 3), ("b", 1, 3), ("y", 0, 2), ("y", 0, 1), ("b", 0, 3), ("y", 0, 3),
    ("s",), ("t", 0),
)
CHIP_ORDER = ((1, 2), (1, 1), (1, 3), (1, 0), (0, 2), (0, 1), (0, 3), (0, 0))


def scale_of(degrees):
    safe = jnp.maximum(degrees, 1).astype(F32)
    return jnp.where(degrees > 0, lax.rsqrt(safe), jnp.float32(0.0))


def down_rows(line, width):
    square = jnp.broadcast_to(line, (BS, BS)).T
    return jnp.concatenate([square] * (width // BS), axis=1) if width > BS else square


def short_has(way, step):
    return step < 3 or (step == 3 and way == 0)


def short_at(way, step):
    return 1 + step + 4 * way


def gather_has(way, step, d):
    return step < 3 or (step == 3 and (d in (0, 1)) == (way == 0))


def short_ring_has(way, step):
    return step > 0 or way == 0


def scatter_has(way, step, d):
    return step > 0 or (d in (2, 0)) == (way == 0)


def kernel(
    feat_h, weight_h, cot_h, deg_h, adj, brow_h, bcol_h, cnt_h,
    act_out, fg_out, wg_out,
    feat, weight, cot, deg, brow, bcol, cnt,
    blocks, turned, src, acc, inv_v, inv_s,
    pair_out, pair_in, chip_out, chip_in, grads,
    part, ring_out, ring_in, last_out, last_in,
    w_half_out, w_half_in, w_piece_out, w_piece_in, w_z, w_y, w_all, w_other,
    short_out, short_in, short_ring_out, short_ring_in,
    in_sem, adj_sem, inv_sem, gy_s, gy_r, gz_s, gz_r, pair_s, pair_r, chip_s, chip_r,
    ag_s, ag_r, fw_s, fw_r, rz_s, rz_r, ry_s, ry_r,
    wh_s, wh_r, wp_s, wp_r, wz_s, wz_r, wy_s, wy_r, wa_s, wa_r, wo_s, wo_r,
    hz_s, hz_r, hy_s, hy_r, kz_s, kz_r, ky_s, ky_r,
):
    row = lax.axis_index("row")
    col = lax.axis_index("col")
    y, z = row // NZ, row % NZ
    chip, core = col // 2, col % 2
    ylo, x = chip // NX, chip % NX

    def at_z(k):
        return (y * NZ + (z + k + NZ) % NZ, col)

    def at_y(d):
        return (((y + d) % NY) * NZ + z, col)

    def chip_at(k):
        dl, dx = CHIP_ORDER[k]
        return ((ylo + dl) % NL) * NX + (x + dx) % NX

    def chip_from(k):
        dl, dx = CHIP_ORDER[k]
        return ((ylo + NL - dl) % NL) * NX + (x + NX - dx) % NX

    def at_chip(k):
        return (row, chip_at(k) * 2 + core)

    sibling = (row, chip * 2 + 1 - core)

    own_line, row_line = col * (NY * NZ) + row, row * (CHIPS * 2) + col
    loads = [
        pltpu.make_async_copy(source, target, in_sem.at[i])
        for i, (source, target) in enumerate(
            (
                (deg_h.at[pl.ds(own_line // 8 * 8, 8)], deg.at[0]), (feat_h, feat), (brow_h, brow), (bcol_h, bcol),
                (cnt_h, cnt), (weight_h, weight), (cot_h, cot),
                (deg_h.at[pl.ds(row_line // 8 * 8, 8)], deg.at[1]),
            )
        )
    ]
    for load in loads:
        load.start()
    adj_copy = pltpu.make_async_copy(adj, blocks.at[pl.ds(0, CAP)], adj_sem)
    adj_copy.start()

    barrier = pltpu.get_barrier_semaphore()
    partners = [at_z(k) for k in range(1, NZ)] + [at_y(d) for d in range(1, NY)]
    partners += [at_chip(k) for k in range(CHIPS - 1)] + [sibling]
    for partner in partners:
        pl.semaphore_signal(barrier, inc=1, device_id=partner, device_id_type=MESH)

    for load in loads[:2]:
        load.wait()
    own_scale = down_rows(scale_of(deg[0, pl.ds(own_line % 8, 1), :]), F)
    src[row] = (feat[...].astype(F32) * own_scale).astype(BF)

    pl.semaphore_wait(barrier, len(partners))

    started = []

    def send(source, target, send_sem, recv_sem, device):
        copy = pltpu.make_async_remote_copy(
            src_ref=source, dst_ref=target, send_sem=send_sem, recv_sem=recv_sem,
            device_id=device, device_id_type=MESH,
        )
        copy.start()
        started.append(copy)

    def arrived(buffer, recv_sem):
        pltpu.make_async_remote_copy(
            src_ref=buffer, dst_ref=buffer, send_sem=recv_sem, recv_sem=recv_sem,
            device_id=sibling, device_id_type=MESH,
        ).wait_recv()

    def origin(way, step, d):
        zz = (z - step + NZ) % NZ if way == 0 else (z + step) % NZ
        return ((y + NY - d) % NY) * NZ + zz

    def tall(r, c):
        return src.at[r, pl.ds(c * G_ROWS, G_ROWS)]

    def short(r):
        return src.at[r, pl.ds(TALL, BS - TALL)]

    def pass_on(c, way, step, d):
        ref = tall(origin(way, step, d), c)
        i = d * G_PIECES + c
        send(ref, ref, gz_s.at[way, step, i], gz_r.at[way, step, i], at_z(1 if way == 0 else -1))

    def short_pass_on(way, step):
        ref = short(origin(way, step, 0))
        send(ref, ref, hz_s.at[way, step], hz_r.at[way, step], at_z(1 if way == 0 else -1))

    def short_spread(i, r):
        for d in (2, 1, 3):
            send(short(r), short(r), hy_s.at[i, d], hy_r.at[i, d], at_y(d))

    for c in range(G_PIECES):
        for d in (1, 3, 2):
            i = d * G_PIECES + c
            send(tall(row, c), tall(row, c), gy_s.at[i], gy_r.at[i], at_y(d))
    for c in range(G_PIECES):
        for way in (0, 1):
            pass_on(c, way, 0, 0)
    for way in (0, 1):
        short_pass_on(way, 0)
    short_spread(0, row)

    for load in loads[2:5]:
        load.wait()
    lane = lax.broadcasted_iota(I32, (1, BS), 1)
    place = jnp.where(lane < cnt[0, 0], brow[...] * 32 + bcol[...], -1)
    place = jnp.broadcast_to(place, (BS, BS)).T
    slot = lax.broadcasted_iota(I32, (BS, BS), 0)
    spot = lax.broadcasted_iota(I32, (BS, BS), 1)
    for q in range(4):
        hit = jnp.where(place == spot + q * BS, slot - CAP, 0)
        inv_v[q : q + 1, :] = jnp.sum(hit, axis=0, keepdims=True) + CAP
    inv_v[4:8, :] = jnp.zeros((4, BS), I32)
    inv_copy = pltpu.make_async_copy(inv_v, inv_s, inv_sem)
    inv_copy.start()
    blocks[CAP] = jnp.zeros((BS, BS), BF)
    turned[CAP] = jnp.zeros((BS, BS), BF)

    def turn(first, last):
        def one(k, carry):
            turned[k] = blocks[k].T
            return carry

        lax.fori_loop(first, last, one, 0)

    def lookup(r, c):
        return inv_s[r // 4, (r % 4) * 32 + c]

    def strip(z_at):
        return jnp.concatenate([src[yy * NZ + z_at] for yy in range(NY)], axis=0)

    def tile_rows(rows, z_at):
        return jnp.concatenate(
            [
                jnp.concatenate([blocks[lookup(r, yy * NZ + z_at)] for yy in range(NY)], axis=1)
                for r in rows
            ],
            axis=0,
        )

    def add_strip(z_at, first):
        def some(g, carry):
            out = jnp.dot(
                tile_rows([g * 4 + i for i in range(4)], z_at), strip(z_at),
                preferred_element_type=F32,
            ).reshape(4, BS, F)
            if first:
                acc[pl.ds(g * 4, 4)] = out
            else:
                acc[pl.ds(g * 4, 4)] += out
            return carry

        lax.fori_loop(0, 4, some, 0)

    def strip_way(i):
        return (0, i) if i <= 4 else (1, i - 4)

    def strip_z(i):
        way, step = strip_way(i)
        return (z - step + NZ) % NZ if way == 0 else (z + step) % NZ

    adj_copy.wait()
    turn(0, CAP)
    inv_copy.wait()
    for what, *of in GATHER:
        if what == "y":
            c, d = of
            arrived(tall(origin(0, 0, d), c), gy_r.at[d * G_PIECES + c])
            for way in (0, 1):
                pass_on(c, way, 0, d)
        elif what == "z":
            c, way, step, d = of
            arrived(tall(origin(way, step + 1, d), c), gz_r.at[way, step, d * G_PIECES + c])
            if gather_has(way, step + 1, d):
                pass_on(c, way, step + 1, d)
        elif what == "b":
            way, step = of
            r = origin(way, step + 1, 0)
            arrived(short(r), hz_r.at[way, step])
            if short_has(way, step + 1):
                short_pass_on(way, step + 1)
            short_spread(short_at(way, step), r)
        elif what == "q":
            i, d = of
            arrived(short(origin(*strip_way(i), d)), hy_r.at[i, d])
        else:
            add_strip(strip_z(of[0]), of[0] == 0)

    far = (z + 4) % NZ
    for ours in (False, True):
        which = core if ours else 1 - core
        for g in (0, 1):
            ks = range(g * 4, g * 4 + 4)
            rows = [chip_at(k) * 2 + which for k in ks]
            out = jnp.dot(tile_rows(rows, far), strip(far), preferred_element_type=F32)
            for i, k in enumerate(ks):
                total = acc[rows[i]] + out[i * BS : (i + 1) * BS]
                if ours:
                    acc[rows[i]] = total
                else:
                    pair_out[k] = total.astype(BF)
            if not ours:
                group = pl.ds(g * 4, 4)
                send(pair_out.at[group], pair_in.at[group], pair_s.at[g], pair_r.at[g], sibling)
    for g in (0, 1):
        group = pl.ds(g * 4, 4)
        arrived(pair_in.at[group], pair_r.at[g])
        for k in range(g * 4, g * 4 + 4):
            total = acc[chip_at(k) * 2 + core] + pair_in[k].astype(F32)
            if k < CHIPS - 1:
                chip_out[k] = total.astype(BF)
                send(chip_out.at[k], chip_in.at[k], chip_s.at[k], chip_r.at[k], at_chip(k))
    for load in loads[5:]:
        load.wait()
    row_scale = down_rows(scale_of(deg[1, pl.ds(row_line % 8, 1), :]), F)
    for k in reversed(range(CHIPS - 1)):
        arrived(chip_in.at[k], chip_r.at[k])
        total = total + chip_in[k].astype(F32)

    propagated = (total * row_scale).astype(BF)
    pre = jnp.dot(propagated, weight[...], preferred_element_type=F32)
    square = pre * pre
    tanh = jnp.tanh(GELU_A * (pre + GELU_B * (square * pre)))
    cdf = 0.5 * (1.0 + tanh)
    slope = cdf + 0.5 * pre * (1.0 - tanh * tanh) * (GELU_A * (1.0 + 3.0 * GELU_B * square))
    pre_grad = (cot[...].astype(F32) * slope).astype(BF)
    back = lax.dot_general(
        pre_grad, weight[...], (((1,), (1,)), ((), ())), preferred_element_type=F32
    )
    grads[col] = (back * row_scale).astype(BF)

    mine = grads.at[col]
    for k in range(CHIPS - 1):
        send(mine, mine, ag_s.at[k], ag_r.at[k], at_chip(k))
    send(mine, mine, fw_s.at[CHIPS - 1], fw_r.at[CHIPS - 1], sibling)

    act_out[...] = (pre * cdf).astype(BF)
    w_local = lax.dot_general(
        propagated, pre_grad, (((0,), (0,)), ((), ())), preferred_element_type=F32
    )
    part[0] = w_local[0:BS]
    part[1] = w_local[BS:F]
    w_half_out[...] = part[1 - core].astype(BF)
    send(w_half_out, w_half_in, wh_s, wh_r, sibling)

    for k in reversed(range(CHIPS - 1)):
        ref = grads.at[chip_from(k) * 2 + core]
        arrived(ref, ag_r.at[k])
        send(ref, ref, fw_s.at[k], fw_r.at[k], sibling)

    arrived(w_half_in, wh_r)
    half = part[core] + w_half_in[...].astype(F32)
    for c in range(CHIPS):
        w_piece_out[c] = half[c * 16 : (c + 1) * 16].astype(BF)
    for k in range(CHIPS - 1):
        send(w_piece_out.at[chip_at(k)], w_piece_in.at[k], wp_s.at[k], wp_r.at[k], at_chip(k))

    for k in reversed(range(CHIPS)):
        arrived(grads.at[chip_from(k) * 2 + 1 - core], fw_r.at[k])

    def back_strip(i, ds):
        way, step = strip_way(i)
        z_at = (z + step) % NZ if way == 0 else (z + NZ - step) % NZ
        lhs = jnp.concatenate(
            [
                jnp.concatenate(
                    [turned[lookup(r, ((y + d) % NY) * NZ + z_at)] for r in range(16)], axis=1
                )
                for d in ds
            ],
            axis=0,
        )
        out = jnp.dot(lhs, grads[...].reshape(16 * BS, F), preferred_element_type=F32)
        for j, d in enumerate(ds):
            part[i * NY + d] = out[j * BS : (j + 1) * BS]

    def w_step(step):
        if step == 0:
            total = w_piece_out[chip].astype(F32)
            for k in range(CHIPS - 1):
                arrived(w_piece_in.at[k], wp_r.at[k])
                total = total + w_piece_in[k].astype(F32)
            w_z[z] = total.astype(BF)
            for k in range(1, NZ):
                send(w_z.at[z], w_z.at[z], wz_s.at[k], wz_r.at[k], at_z(k))
        if step == 1:
            for k in range(1, NZ):
                arrived(w_z.at[(z + NZ - k) % NZ], wz_r.at[k])
            total = w_z[0].astype(F32)
            for k in range(1, NZ):
                total = total + w_z[k].astype(F32)
            w_y[y] = total.astype(BF)
            for d in range(1, NY):
                send(w_y.at[y], w_y.at[y], wy_s.at[d], wy_r.at[d], at_y(d))
        if step == 2:
            for d in range(1, NY):
                arrived(w_y.at[(y + NY - d) % NY], wy_r.at[d])
            total = w_y[0].astype(F32)
            for d in range(1, NY):
                total = total + w_y[d].astype(F32)
            w_all[chip] = total.astype(BF)
            for k in range(CHIPS - 1):
                send(w_all.at[chip], w_all.at[chip], wa_s.at[k], wa_r.at[k], at_chip(k))
        if step == 3:
            for k in range(CHIPS - 1):
                arrived(w_all.at[chip_from(k)], wa_r.at[k])
            send(w_all, w_other, wo_s, wo_r, sibling)

    def short_total(i):
        total = part[i * NY, TALL:BS]
        for d in (1, 3, 2):
            arrived(short_in.at[i, d], ky_r.at[i, d])
            total = total + short_in[i, d].astype(F32)
        return total

    def rows_of(c):
        return slice(c * S_ROWS, (c + 1) * S_ROWS)

    def strip_at(way, step):
        return 4 - step if way == 0 or step == 0 else 8 - step

    for what, *of in SCATTER:
        if what == "c":
            back_strip(of[0], range(NY))
        elif what == "d":
            back_strip(of[0], of[1:])
        elif what == "q":
            i = of[0]
            for d in (2, 1, 3):
                short_out[i, d] = part[i * NY + d, TALL:BS].astype(BF)
                send(short_out.at[i, d], short_in.at[i, d], ky_s.at[i, d], ky_r.at[i, d], at_y(d))
        elif what == "z":
            c, way, step, d = of
            value = part[strip_at(way, step) * NY + d, rows_of(c)]
            rows, i = pl.ds(c * S_ROWS, S_ROWS), d * S_PIECES + c
            if step and scatter_has(way, step - 1, d):
                arrived(ring_in.at[way, step - 1, d, rows], rz_r.at[way, step - 1, i])
                value = value + ring_in[way, step - 1, d, rows_of(c)].astype(F32)
            ring_out[way, step, d, rows_of(c)] = value.astype(BF)
            send(
                ring_out.at[way, step, d, rows], ring_in.at[way, step, d, rows],
                rz_s.at[way, step, i], rz_r.at[way, step, i], at_z(1 if way == 0 else -1),
            )
        elif what == "b":
            way, step = of
            total = short_total(strip_at(way, step))
            if step and short_ring_has(way, step - 1):
                arrived(short_ring_in.at[way, step - 1], kz_r.at[way, step - 1])
                total = total + short_ring_in[way, step - 1].astype(F32)
            short_ring_out[way, step] = total.astype(BF)
            send(
                short_ring_out.at[way, step], short_ring_in.at[way, step],
                kz_s.at[way, step], kz_r.at[way, step], at_z(1 if way == 0 else -1),
            )
        elif what == "w":
            w_step(of[0])
        elif what == "s":
            total = short_total(0)
            for way in (0, 1):
                arrived(short_ring_in.at[way, 3], kz_r.at[way, 3])
                total = total + short_ring_in[way, 3].astype(F32)
            fg_out[TALL:BS, :] = (total * own_scale[TALL:BS]).astype(BF)
        else:
            c, d = of[0], of[1] if what == "y" else 0
            rows, i = pl.ds(c * S_ROWS, S_ROWS), d * S_PIECES + c
            value = part[d, rows_of(c)]
            for way in (0, 1):
                arrived(ring_in.at[way, 3, d, rows], rz_r.at[way, 3, i])
                value = value + ring_in[way, 3, d, rows_of(c)].astype(F32)
            if what == "y":
                last_out[d, rows_of(c)] = value.astype(BF)
                send(last_out.at[d, rows], last_in.at[d, rows], ry_s.at[i], ry_r.at[i], at_y(d))
                continue
            for d in (1, 3, 2):
                arrived(last_in.at[d, rows], ry_r.at[d * S_PIECES + c])
                value = value + last_in[d, rows_of(c)].astype(F32)
            fg_out[rows_of(c), :] = (value * own_scale[rows_of(c)]).astype(BF)

    arrived(w_other, wo_r)
    wg_out[pl.ds(pl.multiple_of(core * BS, BS), BS), :] = w_all[...].astype(F32).reshape(BS, F)
    wg_out[pl.ds(pl.multiple_of((1 - core) * BS, BS), BS), :] = (
        w_other[...].astype(F32).reshape(BS, F)
    )

    for copy in started:
        copy.wait_send()


def per_device(
    features, weight, cotangent, degrees, adj_blocks, block_rows, block_cols, block_count
):
    vmem = pl.BlockSpec(memory_space=pltpu.VMEM)
    dma = pltpu.SemaphoreType.DMA
    block = (BS, F)
    high, low = (TALL, F), (BS - TALL, F)
    scratch = [
        pltpu.VMEM(block, BF),
        pltpu.VMEM((F, F), BF),
        pltpu.VMEM(block, BF),
        pltpu.VMEM((2, 8, BS), I32),
        pltpu.VMEM((1, BS), I32),
        pltpu.VMEM((1, BS), I32),
        pltpu.SMEM((1, 1), I32),
        pltpu.VMEM((CAP + 1, BS, BS), BF),
        pltpu.VMEM((CAP + 1, BS, BS), BF),
        pltpu.VMEM((NY * NZ,) + block, BF),
        pltpu.VMEM((CHIPS * 2,) + block, F32),
        pltpu.VMEM((8, BS), I32),
        pltpu.SMEM((8, BS), I32),
        pltpu.VMEM((CHIPS,) + block, BF),
        pltpu.VMEM((CHIPS,) + block, BF),
        pltpu.VMEM((CHIPS,) + block, BF),
        pltpu.VMEM((CHIPS,) + block, BF),
        pltpu.VMEM((CHIPS * 2,) + block, BF),
        pltpu.VMEM((NZ * NY,) + block, F32),
        pltpu.VMEM((2, 4, NY) + high, BF),
        pltpu.VMEM((2, 4, NY) + high, BF),
        pltpu.VMEM((NY,) + high, BF),
        pltpu.VMEM((NY,) + high, BF),
        pltpu.VMEM(block, BF),
        pltpu.VMEM(block, BF),
        pltpu.VMEM((CHIPS, 16, F), BF),
        pltpu.VMEM((CHIPS, 16, F), BF),
        pltpu.VMEM((NZ, 16, F), BF),
        pltpu.VMEM((NY, 16, F), BF),
        pltpu.VMEM((CHIPS, 16, F), BF),
        pltpu.VMEM((CHIPS, 16, F), BF),
        pltpu.VMEM((NZ, NY) + low, BF),
        pltpu.VMEM((NZ, NY) + low, BF),
        pltpu.VMEM((2, 4) + low, BF),
        pltpu.VMEM((2, 4) + low, BF),
    ]
    sems = [dma((8,)), dma, dma]
    for shape in (
        (NY * G_PIECES,), (2, 4, NY * G_PIECES), (2,), (CHIPS,), (CHIPS,), (CHIPS,),
        (2, 4, NY * S_PIECES), (NY * S_PIECES,),
        None, (CHIPS,), (NZ,), (NY,), (CHIPS,), None,
        (2, 4), (NZ, NY), (2, 4), (NZ, NY),
    ):
        sems += [dma if shape is None else dma(shape)] * 2
    return pl.pallas_call(
        kernel,
        out_shape=(
            pltpu.VMEM(block, BF),
            pltpu.VMEM(block, BF),
            pltpu.VMEM((F, F), F32),
        ),
        in_specs=[pl.BlockSpec(memory_space=pltpu.HBM)] * 8,
        out_specs=(vmem, vmem, vmem),
        scratch_shapes=scratch + sems,
        compiler_params=pltpu.CompilerParams(
            collective_id=0, has_side_effects=True, vmem_limit_bytes=58 * 1024 * 1024
        ),
        cost_estimate=pl.CostEstimate(
            flops=8 * 2048 * 4096 * 256 // 2, bytes_accessed=5 * 1024 * 1024, transcendentals=32768
        ),
        name="layer",
    )(
        features,
        weight,
        cotangent,
        degrees.reshape(-1, BS),
        adj_blocks.reshape(CAP, BS, BS),
        block_rows.reshape(1, CAP),
        block_cols.reshape(1, CAP),
        block_count,
    )


def solution(mesh):
    in_specs = (
        P(("col", "row"), None),
        P(),
        P(("row", "col"), None),
        P(),
        P("row", "col", None, None, None),
        P("row", "col", None),
        P("row", "col", None),
        P("row", "col"),
    )
    out_specs = (P(("row", "col"), None), P(("col", "row"), None), P())
    return jax.shard_map(
        per_device, mesh=mesh, in_specs=in_specs, out_specs=out_specs, check_vma=False
    )
```
